32 devices in a mesh: ctx: 8 (over z, x), head: 4 (over y, core).
Axes of the slice: x: 2, y: 2, z: 4, core: 2. Of those that a mesh axis runs over, the one named last changes fastest.
Arguments:
- queries: bfloat16 [1024, 6144], P('ctx', 'head'), as said below
- key_rows: bfloat16 [1024, 6144], P('ctx', 'head')
- value_rows: bfloat16 [1024, 6144], P('ctx', 'head'), may hold values from -6 to 6
- summary_index: int32 [8], P('ctx'), may hold values from 0 to 15
- out_weight: bfloat16 [6144, 6144], P('head'), may hold values from -0.078125 to 0.078125
- out_grad: bfloat16 [1024, 6144], P('ctx'), may hold values from -6 to 6
Outputs:
- attended: bfloat16 [1024, 6144], P('ctx', 'head')
- grad_query: bfloat16 [1024, 6144], P('ctx', 'head')
- grad_key: bfloat16 [1024, 6144], P('ctx', 'head')
- grad_value: bfloat16 [1024, 6144], P('ctx', 'head')
The draws below stay inside these ranges and needn't reach their ends.
Inputs may be any that keep to these rules, and one draw needn't show every extreme that they name: queries and keys are finite bfloat16 values.
All inputs are finite; a program needn't handle non-finite values.
Results may differ from the reference program's by a relative error of at most 0.018.
Values may be sent and summed in bfloat16 or wider, within the bound.
No kernel may reach another device: no remote copies, remote signals or barrier semaphores. Data moves between devices by JAX's collectives and lax.ppermute only.
A program may use at most 64 MiB of HBM per device.

```python
import jax
import jax.numpy as jnp
from jax import lax

D = 6144
HEADS = 48
HEAD_DIM = 128
STRIDE = 128
SUMMARY = 8
TOKENS = 1024
STRIDES = 8
N_HEAD = 4


def summary_draw(key):
    blocks = STRIDE // SUMMARY
    drawn = jax.random.randint(jax.random.fold_in(key, 15), (STRIDES,), 0, blocks, jnp.int32)
    order = jax.random.permutation(jax.random.fold_in(key, 16), STRIDES)
    drawn = drawn.at[order[0]].set(blocks - 1)
    drawn = drawn.at[order[1]].set(0)
    return drawn


def joint_draw(key):
    width = HEADS * HEAD_DIM
    keys_base = jnp.clip(jax.random.normal(jax.random.fold_in(key, 11), (TOKENS, width), jnp.float32), -6.0, 6.0)
    query_base = jnp.clip(jax.random.normal(jax.random.fold_in(key, 12), (TOKENS, width), jnp.float32), -6.0, 6.0)
    return (query_base, keys_base)


def draw_queries(key, part):
    return joint_draw(key)[0].astype(jnp.bfloat16)


def draw_key_rows(key, part):
    return joint_draw(key)[1].astype(jnp.bfloat16)


def draw_summary_index(key, part):
    return summary_draw(key)


def steps_of(stream_key, shape, split, least, top_value):
    def one(dim, shards_of):
        steps = jax.random.uniform(jax.random.fold_in(jax.random.fold_in(stream_key, 6), dim), (shards_of,), jnp.float32, least / len(split), top_value / len(split))
        return jnp.repeat(jnp.exp(steps), shape[dim] // shards_of).reshape((-1,) + (1,) * (len(shape) - dim - 1))

    loudness = one(*split[0])
    for cut in split[1:]:
        loudness = loudness * one(*cut)
    return loudness


def normal_values(key, extent, deviation, most, shards=(), held_as=jnp.bfloat16):
    loudness = steps_of(key, extent, shards, -0.22, 0.18) if shards else 1.0
    result = jax.random.normal(key, extent, jnp.float32) * deviation * loudness
    return jnp.minimum(jnp.maximum(result, -most), most).astype(held_as)


def setup_inputs(seed: int = 0) -> dict:
    splits = jax.random.split(jax.random.key(seed), 7)
    queries = draw_queries(jax.random.fold_in(splits[6], 71), 0)
    key_rows = draw_key_rows(jax.random.fold_in(splits[6], 71), 0)
    value_rows = normal_values(splits[2], (TOKENS, HEADS * HEAD_DIM), 1.0, 6.0, ((0, 8), (1, 4)))
    summary_index = draw_summary_index(jax.random.fold_in(splits[6], 71), 0)
    out_weight = normal_values(splits[4], (HEADS * HEAD_DIM, D), (HEADS * HEAD_DIM) ** -0.5, 0.078125, ((0, 4),))
    out_grad = normal_values(splits[5], (TOKENS, D), 1.0, 6.0, ((0, 8),))
    return dict(queries=queries, key_rows=key_rows, value_rows=value_rows, summary_index=summary_index, out_weight=out_weight, out_grad=out_grad)


def pick_rows(rows, summary_index):
    blocks = STRIDE // SUMMARY
    width = HEADS * HEAD_DIM
    shaped = rows.reshape(STRIDES, blocks, SUMMARY, width)
    chosen = jnp.take_along_axis(shaped, summary_index.astype(jnp.int32).reshape(STRIDES, 1, 1, 1), axis=1)
    return chosen.reshape(STRIDES * SUMMARY, HEADS, HEAD_DIM)


def reference(queries, key_rows, value_rows, summary_index, out_weight, out_grad):
    scale = HEAD_DIM ** -0.5
    width = HEADS * HEAD_DIM
    blocks = STRIDE // SUMMARY
    slots = STRIDES * SUMMARY
    sum_keys = pick_rows(key_rows, summary_index).astype(jnp.float32)
    sum_vals = pick_rows(value_rows, summary_index).astype(jnp.float32)
    dattn_all = jnp.dot(out_grad, out_weight.T, preferred_element_type=jnp.float32).astype(jnp.bfloat16)
    causal = jnp.arange(STRIDE)[:, None] >= jnp.arange(STRIDE)[None, :]
    slot_block = jnp.arange(slots) // SUMMARY

    def step(carry, inputs):
        block, qs, ks, vs, das = inputs
        qf = qs.astype(jnp.float32)
        kf = ks.astype(jnp.float32)
        vf = vs.astype(jnp.float32)
        daf = das.astype(jnp.float32)
        visible = (slot_block < block)[None, None, :]
        s_loc = jnp.einsum('qhd,khd->hqk', qf, kf) * scale
        s_loc = jnp.where(causal[None], s_loc, -jnp.inf)
        s_sum = jnp.einsum('qhd,khd->hqk', qf, sum_keys) * scale
        s_sum = jnp.where(visible, s_sum, -jnp.inf)
        top = jnp.maximum(jnp.max(s_loc, axis=-1, keepdims=True), jnp.max(s_sum, axis=-1, keepdims=True))
        e_loc = jnp.exp(s_loc - top)
        e_sum = jnp.exp(s_sum - top)
        total = jnp.sum(e_loc, axis=-1, keepdims=True) + jnp.sum(e_sum, axis=-1, keepdims=True)
        p_loc = e_loc / total
        p_sum = e_sum / total
        pb_loc = p_loc.astype(jnp.bfloat16).astype(jnp.float32)
        pb_sum = p_sum.astype(jnp.bfloat16).astype(jnp.float32)
        attn = (jnp.einsum('hqk,khd->qhd', pb_loc, vf) + jnp.einsum('hqk,khd->qhd', pb_sum, sum_vals)).astype(jnp.bfloat16)
        dp_loc = jnp.einsum('qhd,khd->hqk', daf, vf)
        dp_sum = jnp.einsum('qhd,khd->hqk', daf, sum_vals)
        delta = jnp.sum(p_loc * dp_loc, axis=-1, keepdims=True) + jnp.sum(p_sum * dp_sum, axis=-1, keepdims=True)
        ds_loc = (p_loc * (dp_loc - delta)).astype(jnp.bfloat16).astype(jnp.float32)
        ds_sum = (p_sum * (dp_sum - delta)).astype(jnp.bfloat16).astype(jnp.float32)
        grad_q = (scale * (jnp.einsum('hqk,khd->qhd', ds_loc, kf) + jnp.einsum('hqk,khd->qhd', ds_sum, sum_keys))).astype(jnp.bfloat16)
        dk_loc = scale * jnp.einsum('hqk,qhd->khd', ds_loc, qf)
        dv_loc = jnp.einsum('hqk,qhd->khd', pb_loc, daf)
        new_k = carry[0] + scale * jnp.einsum('hqk,qhd->khd', ds_sum, qf)
        new_v = carry[1] + jnp.einsum('hqk,qhd->khd', pb_sum, daf)
        return (new_k, new_v), (attn, grad_q, dk_loc, dv_loc)

    shape4 = (STRIDES, STRIDE, HEADS, HEAD_DIM)
    xs = (jnp.arange(STRIDES).astype(jnp.int32), queries.reshape(shape4), key_rows.reshape(shape4),
          value_rows.reshape(shape4), dattn_all.reshape(shape4))
    zeros = jnp.zeros((slots, HEADS, HEAD_DIM), jnp.float32)
    (sum_dk, sum_dv), (attn, grad_q, dk_loc, dv_loc) = lax.scan(step, (zeros, zeros), xs)
    attn = attn.reshape(TOKENS, width)

    group_cols = width // N_HEAD
    attn_groups = attn.reshape(TOKENS, N_HEAD, group_cols).transpose(1, 0, 2)
    weight_groups = out_weight.reshape(N_HEAD, group_cols, D)

    def add_group(total, pieces):
        term = jnp.dot(pieces[0], pieces[1], preferred_element_type=jnp.float32)
        rounded = lax.optimization_barrier(term.astype(jnp.bfloat16)).astype(jnp.float32)
        return total + rounded, None

    projected, unused = lax.scan(add_group, jnp.zeros((TOKENS, D), jnp.float32), (attn_groups, weight_groups))
    attended = projected.astype(jnp.bfloat16)
    onehot = (jnp.arange(blocks)[None, :] == summary_index[:, None]).astype(jnp.float32)

    def spread(values):
        placed = onehot[:, :, None, None] * values.reshape(STRIDES, 1, SUMMARY, width)
        return placed.reshape(TOKENS, width)

    grad_key = (dk_loc.reshape(TOKENS, width) + spread(sum_dk)).astype(jnp.bfloat16)
    grad_value = (dv_loc.reshape(TOKENS, width) + spread(sum_dv)).astype(jnp.bfloat16)
    return attended, grad_q.reshape(TOKENS, width), grad_key, grad_value
```

```python
import jax
import jax.numpy as jnp
from jax import lax
from jax.experimental import pallas as pl
from jax.experimental.pallas import tpu as pltpu
from jax.sharding import PartitionSpec as P

HEAD_DIM = 128
STRIDE = 128
SUMMARY = 8
PAIR = 2 * SUMMARY
SCALE = HEAD_DIM ** (-0.5)
NT = (((1,), (1,)), ((), ()))
NN = (((1,), (0,)), ((), ()))
TN = (((0,), (0,)), ((), ()))
BF16 = jnp.bfloat16
F32 = jnp.float32
VMEM_LIMIT = 30 * 1024 * 1024


def dot(a, b, dims):
    return lax.dot_general(a, b, dims, preferred_element_type=F32)


def call(body, outs, *args, smem=0, scratch=(), flops=0, moved=0):
    vmem = pl.BlockSpec(memory_space=pltpu.VMEM)
    specs = [pl.BlockSpec(memory_space=pltpu.SMEM)] * smem + [vmem] * (len(args) - smem)
    return pl.pallas_call(
        body,
        in_specs=specs,
        out_specs=[vmem] * len(outs),
        out_shape=[jax.ShapeDtypeStruct(shape, dtype) for shape, dtype in outs],
        scratch_shapes=scratch,
        compiler_params=pltpu.CompilerParams(vmem_limit_bytes=VMEM_LIMIT),
        cost_estimate=pl.CostEstimate(flops=flops, bytes_accessed=moved, transcendentals=0),
    )(*args)


def swap(value, axis, mask):
    return lax.ppermute(value, axis, [(i, i ^ mask) for i in range(lax.axis_size(axis))])


def pick_kernel(index_ref, k_ref, v_ref, own_ref):
    index = index_ref[0]
    start = pl.multiple_of((index // 2) * PAIR, PAIR)
    upper = index % 2 == 1
    k = k_ref[pl.ds(start, PAIR), :].astype(F32)
    v = v_ref[pl.ds(start, PAIR), :].astype(F32)
    k = jnp.where(upper, k[SUMMARY:], k[:SUMMARY])
    v = jnp.where(upper, v[SUMMARY:], v[:SUMMARY])
    own_ref[...] = jnp.concatenate([k, v], axis=0).astype(BF16)


def dattn_kernel(g_ref, w_ref, da_ref):
    width = da_ref.shape[1]
    step = min(256, width)
    for at in range(0, width, step):
        da_ref[:, at : at + step] = dot(g_ref[...], w_ref[at : at + step, :], NT).astype(BF16)


def head_cols(head):
    return slice(head * HEAD_DIM, (head + 1) * HEAD_DIM)


def stacked(refs, cols):
    return jnp.concatenate([ref[:, cols] for ref in refs], axis=0)


def forward_kernel(place_ref, q_ref, k_ref, v_ref, *rest):
    *pieces, attn_ref, p_ref = rest
    place = place_ref[0]
    rows = q_ref.shape[0]
    heads = q_ref.shape[1] // HEAD_DIM
    others = len(pieces)
    slots = others * SUMMARY
    causal = lax.broadcasted_iota(jnp.int32, (rows, rows), 0) <= lax.broadcasted_iota(
        jnp.int32, (rows, rows), 1
    )
    block = lax.broadcasted_iota(jnp.int32, (slots, rows), 0) // SUMMARY + 1
    visible = (block ^ place) < place
    for head in range(heads):
        cols = head_cols(head)
        q = q_ref[:, cols]
        v = v_ref[:, cols]
        both = stacked(pieces, cols)
        s_loc = dot(k_ref[:, cols], q, NT) * SCALE
        s_sum = dot(both, q, NT) * SCALE
        s_sum = s_sum.reshape(others, PAIR, rows)[:, :SUMMARY].reshape(slots, rows)
        s_loc = jnp.where(causal, s_loc, -jnp.inf)
        s_sum = jnp.where(visible, s_sum, -jnp.inf)
        top = jnp.maximum(
            jnp.max(s_loc, axis=0, keepdims=True), jnp.max(s_sum, axis=0, keepdims=True)
        )
        e_loc = jnp.exp(s_loc - top)
        e_sum = jnp.exp(s_sum - top)
        total = jnp.sum(e_loc, axis=0, keepdims=True) + jnp.sum(e_sum, axis=0, keepdims=True)
        share = 1.0 / total
        p_loc = e_loc * share
        p_sum = e_sum * share
        p_ref[head, :rows, :] = p_loc
        p_ref[head, rows:, :] = p_sum
        at_vals = jnp.concatenate(
            [jnp.zeros((others, SUMMARY, rows), F32), p_sum.reshape(others, SUMMARY, rows)], axis=1
        ).reshape(others * PAIR, rows)
        p_all = jnp.concatenate([p_loc.astype(BF16), at_vals.astype(BF16)], axis=0)
        attn_ref[:, cols] = dot(p_all, jnp.concatenate([v, both], axis=0), TN).astype(BF16)


def score_grad_kernel(q_ref, v_ref, da_ref, p_ref, *rest):
    *pieces, pb_ref, ds_ref, term_ref = rest
    rows = q_ref.shape[0]
    heads = q_ref.shape[1] // HEAD_DIM
    others = len(pieces)
    slots = others * SUMMARY
    for head in range(heads):
        cols = head_cols(head)
        q = q_ref[:, cols]
        da = da_ref[:, cols]
        both = stacked(pieces, cols)
        dp_loc = dot(v_ref[:, cols], da, NT)
        dp_sum = dot(both, da, NT)
        dp_sum = dp_sum.reshape(others, PAIR, rows)[:, SUMMARY:].reshape(slots, rows)
        p_loc = p_ref[head, :rows, :]
        p_sum = p_ref[head, rows:, :]
        delta = jnp.sum(p_loc * dp_loc, axis=0, keepdims=True) + jnp.sum(
            p_sum * dp_sum, axis=0, keepdims=True
        )
        ds_loc = p_loc * (dp_loc - delta)
        ds_sum = (p_sum * (dp_sum - delta)).reshape(others, SUMMARY, rows)
        empty = jnp.zeros((others, SUMMARY, rows), F32)
        at_keys = jnp.concatenate([ds_sum, empty], axis=1).reshape(others * PAIR, rows).astype(BF16)
        at_vals = jnp.concatenate([empty, p_sum.reshape(others, SUMMARY, rows)], axis=1)
        at_vals = at_vals.reshape(others * PAIR, rows).astype(BF16)
        pb_ref[head] = p_loc.astype(BF16)
        ds_ref[head, :rows, :] = ds_loc.astype(BF16)
        ds_ref[head, rows:, :] = at_keys
        term = dot(at_keys, q, NN) * SCALE + dot(at_vals, da, NN)
        term_ref[:, :, cols] = term.astype(BF16).reshape(others, PAIR, HEAD_DIM)


def input_grad_kernel(q_ref, k_ref, da_ref, pb_ref, ds_ref, *rest):
    *pieces, dq_ref, dk_ref, dv_ref = rest
    rows = q_ref.shape[0]
    heads = q_ref.shape[1] // HEAD_DIM
    for head in range(heads):
        cols = head_cols(head)
        keys = jnp.concatenate([k_ref[:, cols], stacked(pieces, cols)], axis=0)
        ds = ds_ref[head]
        dq_ref[:, cols] = (dot(ds, keys, TN) * SCALE).astype(BF16)
        dk_ref[:, cols] = dot(ds[:rows], q_ref[:, cols], NN) * SCALE
        dv_ref[:, cols] = dot(pb_ref[head], da_ref[:, cols], NN)


def project_kernel(offsets_ref, attn_ref, w_ref, send_ref, keep_ref):
    width = send_ref.shape[1]
    step = 768 if width % 768 == 0 else width
    for which, out_ref in enumerate((send_ref, keep_ref)):
        for at in range(0, width, step):
            start = pl.multiple_of(offsets_ref[which] + at, HEAD_DIM)
            out_ref[:, at : at + step] = dot(
                attn_ref[...], w_ref[:, pl.ds(start, step)], NN
            ).astype(BF16)


def join_kernel(keep_ref, came_ref, out_ref):
    out_ref[...] = (keep_ref[...].astype(F32) + came_ref[...].astype(F32)).astype(BF16)


def attended_kernel(*refs):
    *parts, out_ref = refs
    total = parts[0][...].astype(F32)
    for part in parts[1:]:
        total = total + part[...].astype(F32)
    out_ref[...] = total.astype(BF16)


def final_kernel(index_ref, dk_ref, dv_ref, *rest):
    *terms, gk_ref, gv_ref = rest
    index = index_ref[0]
    total = terms[0][...].astype(F32)
    for term in terms[1:]:
        total = total + term[...].astype(F32)
    gk_ref[...] = dk_ref[...].astype(BF16)
    gv_ref[...] = dv_ref[...].astype(BF16)
    start = pl.multiple_of((index // 2) * PAIR, PAIR)
    upper = index % 2 == 1
    for ref, out_ref, add in (
        (dk_ref, gk_ref, total[:SUMMARY]),
        (dv_ref, gv_ref, total[SUMMARY:]),
    ):
        low = jnp.where(upper, 0.0, add)
        high = jnp.where(upper, add, 0.0)
        part = ref[pl.ds(start, PAIR), :] + jnp.concatenate([low, high], axis=0)
        out_ref[pl.ds(start, PAIR), :] = part.astype(BF16)


def on_device(queries, key_rows, value_rows, summary_index, out_weight, out_grad):
    rows, width = queries.shape
    heads = width // HEAD_DIM
    shards = lax.axis_size("ctx")
    ranks = lax.axis_size("head")
    place = lax.axis_index("ctx")
    rank = lax.axis_index("head")
    others = shards - 1
    depth = out_weight.shape[1]
    tall = rows + others * PAIR
    place_arr = place.reshape(1)

    (own,) = call(pick_kernel, [((PAIR, width), BF16)], summary_index, key_rows, value_rows, smem=1)
    pieces = {0: own, 1: swap(own, "ctx", 1)}
    for mask in range(2, shards, 2):
        pieces[mask] = swap(own, "ctx", mask)
    for mask in range(2, shards, 2):
        pieces[mask + 1] = swap(pieces[mask], "ctx", 1)
    pieces = [pieces[mask] for mask in range(1, shards)]

    big = 2 * rows * width * depth
    (dattn,) = call(
        dattn_kernel, [((rows, width), BF16)], out_grad, out_weight, flops=2 * big, moved=width * depth * 2
    )
    small = 2 * heads * tall * rows * HEAD_DIM
    attn, probs = call(
        forward_kernel,
        [((rows, width), BF16), ((heads, rows + others * SUMMARY, rows), F32)],
        place_arr, queries, key_rows, value_rows, *pieces,
        smem=1, flops=8 * small,
    )

    def project(mask):
        base = (rank ^ mask) // 2 * 2 * width
        core = rank % 2
        offsets = jnp.stack([base + (1 - core) * width, base + core * width]).astype(jnp.int32)
        return call(
            project_kernel,
            [((rows, width), BF16), ((rows, width), BF16)],
            offsets, attn, out_weight,
            smem=1, flops=4 * 2 * rows * width * width,
        )

    came = []
    for mask in range(2, ranks, 2):
        send, keep = project(mask)
        (joined,) = call(join_kernel, [((rows, width), BF16)], keep, swap(send, "head", 1))
        came.append(swap(joined, "head", mask))

    pb, ds, terms = call(
        score_grad_kernel,
        [((heads, rows, rows), BF16), ((heads, tall, rows), BF16), ((others, PAIR, width), BF16)],
        queries, value_rows, dattn, probs, *pieces,
        flops=8 * small,
    )
    returned = [swap(terms[mask - 1], "ctx", mask) for mask in range(1, shards)]
    send, keep = project(0)
    came = [keep, swap(send, "head", 1)] + came
    grad_query, dk, dv = call(
        input_grad_kernel,
        [((rows, width), BF16), ((rows, width), F32), ((rows, width), F32)],
        queries, key_rows, dattn, pb, ds, *pieces,
        flops=8 * small,
    )
    grad_key, grad_value = call(
        final_kernel, [((rows, width), BF16), ((rows, width), BF16)], summary_index, dk, dv, *returned, smem=1
    )
    (attended,) = call(attended_kernel, [((rows, width), BF16)], *came)
    return (attended, grad_query, grad_key, grad_value)


def solution(mesh):
    return jax.shard_map(
        on_device,
        mesh=mesh,
        in_specs=(
            P("ctx", "head"),
            P("ctx", "head"),
            P("ctx", "head"),
            P("ctx"),
            P("head", None),
            P("ctx", None),
        ),
        out_specs=(P("ctx", "head"), P("ctx", "head"), P("ctx", "head"), P("ctx", "head")),
        check_vma=False,
    )
```

```python
import functools

import jax
import jax.numpy as jnp
from jax import lax
from jax.experimental import pallas as pl
from jax.experimental.pallas import tpu as pltpu
from jax.sharding import PartitionSpec as P

HEAD_DIM = 128
STRIDE = 128
SUMMARY = 8
PAIR = 2 * SUMMARY
SCALE = HEAD_DIM ** (-0.5)
NT = (((1,), (1,)), ((), ()))
NN = (((1,), (0,)), ((), ()))
TN = (((0,), (0,)), ((), ()))
BF16 = jnp.bfloat16
F32 = jnp.float32
VMEM_LIMIT = 12 * 1024 * 1024


def dot(a, b, dims):
    return lax.dot_general(a, b, dims, preferred_element_type=F32)


def call(body, outs, *args, smem=0, hbm=0, scratch=(), flops=0, moved=0):
    vmem = pl.BlockSpec(memory_space=pltpu.VMEM)
    specs = [pl.BlockSpec(memory_space=pltpu.SMEM)] * smem
    specs += [pl.BlockSpec(memory_space=pltpu.HBM)] * hbm
    specs += [vmem] * (len(args) - len(specs))
    return pl.pallas_call(
        body,
        in_specs=specs,
        out_specs=[vmem] * len(outs),
        out_shape=[jax.ShapeDtypeStruct(shape, dtype) for shape, dtype in outs],
        scratch_shapes=scratch,
        compiler_params=pltpu.CompilerParams(vmem_limit_bytes=VMEM_LIMIT),
        cost_estimate=pl.CostEstimate(flops=flops, bytes_accessed=moved, transcendentals=0),
    )(*args)


def swap(value, axis, mask):
    return lax.ppermute(value, axis, [(i, i ^ mask) for i in range(lax.axis_size(axis))])


def pick_kernel(index_ref, k_ref, v_ref, own_ref, k_rows, v_rows, sems):
    index = index_ref[0]
    start = pl.multiple_of((index // 2) * PAIR, PAIR)
    upper = index % 2 == 1
    copies = [
        pltpu.make_async_copy(k_ref.at[pl.ds(start, PAIR), :], k_rows, sems.at[0]),
        pltpu.make_async_copy(v_ref.at[pl.ds(start, PAIR), :], v_rows, sems.at[1]),
    ]
    for copy in copies:
        copy.start()
    for copy in copies:
        copy.wait()
    k = k_rows[...].astype(F32)
    v = v_rows[...].astype(F32)
    k = jnp.where(upper, k[SUMMARY:], k[:SUMMARY])
    v = jnp.where(upper, v[SUMMARY:], v[:SUMMARY])
    own_ref[...] = jnp.concatenate([k, v], axis=0).astype(BF16)


def local_kernel(first, q_ref, k_ref, v_ref, g_ref, w_ref, da_ref, s_ref, dp_ref):
    rows = q_ref.shape[0]
    heads = da_ref.shape[1] // HEAD_DIM
    group = 2 if heads % 2 == 0 else 1
    causal = lax.broadcasted_iota(jnp.int32, (rows, rows), 0) <= lax.broadcasted_iota(
        jnp.int32, (rows, rows), 1
    )
    for at in range(0, heads, group):
        start = (first + at) * HEAD_DIM
        turned = dot(w_ref[start : start + group * HEAD_DIM, :], g_ref[...], NT).astype(BF16)
        da_ref[:, at * HEAD_DIM : (at + group) * HEAD_DIM] = turned.T
        for head in range(at, at + group):
            cols = head_cols(first + head)
            s_loc = dot(k_ref[:, cols], q_ref[:, cols], NT) * SCALE
            s_ref[head] = jnp.where(causal, s_loc, -jnp.inf)
            dp_ref[head] = dot(v_ref[:, cols], turned[head_cols(head - at)], NN)


def head_cols(head):
    return slice(head * HEAD_DIM, (head + 1) * HEAD_DIM)


def of_head(refs, head):
    each = refs[0].shape[0]
    return refs[head // each][head % each]


def part_cols(refs, head):
    each = refs[0].shape[1] // HEAD_DIM
    return refs[head // each][:, head_cols(head % each)]


def stacked(refs, cols):
    return jnp.concatenate([ref[:, cols] for ref in refs], axis=0)


def forward_kernel(parts, q_ref, v_ref, *rest):
    *ins, attn_ref, p_ref = rest
    s_refs, pieces = ins[:parts], ins[parts:]
    place = lax.axis_index("ctx")
    rows = q_ref.shape[0]
    heads = q_ref.shape[1] // HEAD_DIM
    others = len(pieces)
    slots = others * SUMMARY
    block = lax.broadcasted_iota(jnp.int32, (slots, rows), 0) // SUMMARY + 1
    visible = (block ^ place) < place
    for head in range(heads):
        cols = head_cols(head)
        both = stacked(pieces, cols)
        s_loc = of_head(s_refs, head)
        s_sum = dot(both, q_ref[:, cols], NT) * SCALE
        s_sum = s_sum.reshape(others, PAIR, rows)[:, :SUMMARY].reshape(slots, rows)
        s_sum = jnp.where(visible, s_sum, -jnp.inf)
        top = jnp.maximum(
            jnp.max(s_loc, axis=0, keepdims=True), jnp.max(s_sum, axis=0, keepdims=True)
        )
        e_loc = jnp.exp(s_loc - top)
        e_sum = jnp.exp(s_sum - top)
        total = jnp.sum(e_loc, axis=0, keepdims=True) + jnp.sum(e_sum, axis=0, keepdims=True)
        share = 1.0 / total
        p_loc = e_loc * share
        p_sum = e_sum * share
        p_ref[head, :rows, :] = p_loc
        p_ref[head, rows:, :] = p_sum
        at_vals = jnp.concatenate(
            [jnp.zeros((others, SUMMARY, rows), F32), p_sum.reshape(others, SUMMARY, rows)], axis=1
        ).reshape(others * PAIR, rows)
        p_all = jnp.concatenate([p_loc.astype(BF16), at_vals.astype(BF16)], axis=0)
        values = jnp.concatenate([v_ref[:, cols], both], axis=0)
        attn_ref[:, cols] = dot(p_all, values, TN).astype(BF16)


def score_grad_kernel(parts, q_ref, p_ref, *rest):
    da_refs, dp_refs, rest = rest[:parts], rest[parts : 2 * parts], rest[2 * parts :]
    others = (len(rest) - 2) // 2
    pieces, (pb_ref, ds_ref), term_refs = rest[:others], rest[others : others + 2], rest[others + 2 :]
    rows = q_ref.shape[0]
    heads = q_ref.shape[1] // HEAD_DIM
    slots = others * SUMMARY
    for head in range(heads):
        cols = head_cols(head)
        q = q_ref[:, cols]
        da = part_cols(da_refs, head)
        dp_loc = of_head(dp_refs, head)
        dp_sum = dot(stacked(pieces, cols), da, NT)
        dp_sum = dp_sum.reshape(others, PAIR, rows)[:, SUMMARY:].reshape(slots, rows)
        p_loc = p_ref[head, :rows, :]
        p_sum = p_ref[head, rows:, :]
        delta = jnp.sum(p_loc * dp_loc, axis=0, keepdims=True) + jnp.sum(
            p_sum * dp_sum, axis=0, keepdims=True
        )
        ds_loc = p_loc * (dp_loc - delta)
        ds_sum = (p_sum * (dp_sum - delta)).reshape(others, SUMMARY, rows)
        empty = jnp.zeros((others, SUMMARY, rows), F32)
        at_keys = jnp.concatenate([ds_sum, empty], axis=1).reshape(others * PAIR, rows).astype(BF16)
        at_vals = jnp.concatenate([empty, p_sum.reshape(others, SUMMARY, rows)], axis=1)
        at_vals = at_vals.reshape(others * PAIR, rows).astype(BF16)
        pb_ref[head] = p_loc.astype(BF16)
        ds_ref[head, :rows, :] = ds_loc.astype(BF16)
        ds_ref[head, rows:, :] = at_keys
        term = dot(at_keys, q, NN) * SCALE + dot(at_vals, da, NN)
        for at, term_ref in enumerate(term_refs):
            term_ref[:, cols] = term[at * PAIR : (at + 1) * PAIR].astype(BF16)


def input_grad_kernel(parts, q_ref, k_ref, pb_ref, ds_ref, *rest):
    *ins, dq_ref, dk_ref, dv_ref = rest
    da_refs, pieces = ins[:parts], ins[parts:]
    rows = q_ref.shape[0]
    heads = q_ref.shape[1] // HEAD_DIM
    for head in range(heads):
        cols = head_cols(head)
        keys = jnp.concatenate([k_ref[:, cols], stacked(pieces, cols)], axis=0)
        ds = ds_ref[head]
        dq_ref[:, cols] = (dot(ds, keys, TN) * SCALE).astype(BF16)
        dk_ref[:, cols] = dot(ds[:rows], q_ref[:, cols], NN) * SCALE
        dv_ref[:, cols] = dot(pb_ref[head], part_cols(da_refs, head), NN)


def project_kernel(mask, attn_ref, w_ref, send_ref, keep_ref):
    width = send_ref.shape[1]
    rank = lax.axis_index("head")
    target = rank ^ mask
    for goal, out_ref in ((target ^ 1, send_ref), (target, keep_ref)):
        start = pl.multiple_of(goal * width, HEAD_DIM)
        out_ref[...] = dot(attn_ref[...], w_ref[:, pl.ds(start, width)], NN).astype(BF16)


def join_kernel(keep_ref, came_ref, out_ref):
    out_ref[...] = (keep_ref[...].astype(F32) + came_ref[...].astype(F32)).astype(BF16)


def attended_kernel(*refs):
    *parts, out_ref = refs
    total = parts[0][...].astype(F32)
    for part in parts[1:]:
        total = total + part[...].astype(F32)
    out_ref[...] = total.astype(BF16)


def final_kernel(index_ref, dk_ref, dv_ref, *rest):
    *terms, gk_ref, gv_ref = rest
    index = index_ref[0]
    total = terms[0][...].astype(F32)
    for term in terms[1:]:
        total = total + term[...].astype(F32)
    gk_ref[...] = dk_ref[...].astype(BF16)
    gv_ref[...] = dv_ref[...].astype(BF16)
    start = pl.multiple_of((index // 2) * PAIR, PAIR)
    upper = index % 2 == 1
    for ref, out_ref, add in (
        (dk_ref, gk_ref, total[:SUMMARY]),
        (dv_ref, gv_ref, total[SUMMARY:]),
    ):
        low = jnp.where(upper, 0.0, add)
        high = jnp.where(upper, add, 0.0)
        part = ref[pl.ds(start, PAIR), :] + jnp.concatenate([low, high], axis=0)
        out_ref[pl.ds(start, PAIR), :] = part.astype(BF16)


def on_device(queries, key_rows, value_rows, summary_index, out_weight, out_grad):
    rows, width = queries.shape
    heads = width // HEAD_DIM
    shards = lax.axis_size("ctx")
    ranks = lax.axis_size("head")
    others = shards - 1
    depth = out_weight.shape[1]
    tall = rows + others * PAIR

    (own,) = call(
        pick_kernel,
        [((PAIR, width), BF16)],
        summary_index, key_rows, value_rows,
        smem=1, hbm=2, flops=2 * 10**10,
        scratch=[pltpu.VMEM((PAIR, width), BF16)] * 2 + [pltpu.SemaphoreType.DMA((2,))],
    )
    pieces = {0: own, 1: swap(own, "ctx", 1)}
    for mask in range(2, shards, 2):
        pieces[mask] = swap(own, "ctx", mask)

    big = 2 * rows * width * depth
    parts = 2 if heads % 2 == 0 else 1
    each = heads // parts
    das, scores, dps = [], [], []
    gates = (queries, out_grad)
    for first in range(0, heads, each):
        da, score, dp = call(
            functools.partial(local_kernel, first),
            [((rows, each * HEAD_DIM), BF16)] + [((each, rows, rows), F32)] * 2,
            gates[0], key_rows, value_rows, gates[1], out_weight,
            flops=3 * big, moved=width * depth,
        )
        das.append(da)
        scores.append(score)
        dps.append(dp)
        if first == 0:
            evens = [pieces[mask] for mask in range(2, shards, 2)]
            evens, *gates = lax.optimization_barrier((evens, *gates))
            for mask, piece in zip(range(2, shards, 2), evens):
                pieces[mask] = piece
                pieces[mask + 1] = swap(piece, "ctx", 1)
    pieces, das = lax.optimization_barrier(([pieces[mask] for mask in range(1, shards)], das))

    small = 2 * heads * tall * rows * HEAD_DIM
    attn, probs = call(
        functools.partial(forward_kernel, parts),
        [((rows, width), BF16), ((heads, rows + others * SUMMARY, rows), F32)],
        queries, value_rows, *scores, *pieces,
        flops=8 * small,
    )

    def project(mask):
        return call(
            functools.partial(project_kernel, mask),
            [((rows, width), BF16), ((rows, width), BF16)],
            attn, out_weight,
            flops=4 * rows * width * width, moved=4 * width * width,
        )

    came = []
    for mask in range(2, ranks, 2):
        send, keep = project(mask)
        (joined,) = call(join_kernel, [((rows, width), BF16)], keep, swap(send, "head", 1))
        came.append(swap(joined, "head", mask))

    pb, ds, *terms = call(
        functools.partial(score_grad_kernel, parts),
        [((heads, rows, rows), BF16), ((heads, tall, rows), BF16)]
        + [((PAIR, width), BF16)] * others,
        queries, probs, *das, *dps, *pieces,
        flops=8 * small,
    )
    returned = [swap(terms[mask - 1], "ctx", mask) for mask in range(1, shards)]
    send, keep = project(0)
    came = [keep, swap(send, "head", 1)] + came
    grad_query, dk, dv = call(
        functools.partial(input_grad_kernel, parts),
        [((rows, width), BF16), ((rows, width), F32), ((rows, width), F32)],
        queries, key_rows, pb, ds, *das, *pieces,
        flops=8 * small,
    )
    grad_key, grad_value = call(
        final_kernel, [((rows, width), BF16), ((rows, width), BF16)], summary_index, dk, dv, *returned, smem=1
    )
    (attended,) = call(attended_kernel, [((rows, width), BF16)], *came)
    return (attended, grad_query, grad_key, grad_value)


def solution(mesh):
    return jax.shard_map(
        on_device,
        mesh=mesh,
        in_specs=(
            P("ctx", "head"),
            P("ctx", "head"),
            P("ctx", "head"),
            P("ctx"),
            P("head", None),
            P("ctx", None),
        ),
        out_specs=(P("ctx", "head"), P("ctx", "head"), P("ctx", "head"), P("ctx", "head")),
        check_vma=False,
    )
```

```python
import functools

import jax
import jax.numpy as jnp
from jax import lax
from jax.experimental import pallas as pl
from jax.experimental.pallas import tpu as pltpu
from jax.sharding import PartitionSpec as P

HEAD_DIM = 128
STRIDE = 128
SUMMARY = 8
PAIR = 2 * SUMMARY
SCALE = HEAD_DIM ** (-0.5)
NT = (((1,), (1,)), ((), ()))
NN = (((1,), (0,)), ((), ()))
TN = (((0,), (0,)), ((), ()))
BF16 = jnp.bfloat16
F32 = jnp.float32
VMEM_LIMIT = 12 * 1024 * 1024


def dot(a, b, dims):
    return lax.dot_general(a, b, dims, preferred_element_type=F32)


def call(body, outs, *args, smem=0, hbm=0, scratch=(), flops=0, moved=0):
    vmem = pl.BlockSpec(memory_space=pltpu.VMEM)
    specs = [pl.BlockSpec(memory_space=pltpu.SMEM)] * smem
    specs += [pl.BlockSpec(memory_space=pl.ANY)] * hbm
    specs += [vmem] * (len(args) - len(specs))
    return pl.pallas_call(
        body,
        in_specs=specs,
        out_specs=[vmem] * len(outs),
        out_shape=[jax.ShapeDtypeStruct(shape, dtype) for shape, dtype in outs],
        scratch_shapes=scratch,
        compiler_params=pltpu.CompilerParams(vmem_limit_bytes=VMEM_LIMIT),
        cost_estimate=pl.CostEstimate(flops=flops, bytes_accessed=moved, transcendentals=0),
    )(*args)


def swap(value, axis, mask):
    return lax.ppermute(value, axis, [(i, i ^ mask) for i in range(lax.axis_size(axis))])


def pick_kernel(index_ref, q_ref, k_ref, v_ref, own_ref, q_out, k_out, v_out, sems):
    copies = [
        pltpu.make_async_copy(source, target, sems.at[i])
        for i, (source, target) in enumerate(((k_ref, k_out), (v_ref, v_out), (q_ref, q_out)))
    ]
    for copy in copies:
        copy.start()
    index = index_ref[0]
    start = pl.multiple_of((index // 2) * PAIR, PAIR)
    upper = index % 2 == 1
    copies[0].wait()
    copies[1].wait()
    k = k_out[pl.ds(start, PAIR), :].astype(F32)
    v = v_out[pl.ds(start, PAIR), :].astype(F32)
    k = jnp.where(upper, k[SUMMARY:], k[:SUMMARY])
    v = jnp.where(upper, v[SUMMARY:], v[:SUMMARY])
    own_ref[...] = jnp.concatenate([k, v], axis=0).astype(BF16)
    copies[2].wait()


def gather_kernel(*refs):
    *parts, out_ref = refs
    for at, part in enumerate(parts):
        out_ref[at * PAIR : (at + 1) * PAIR, :] = part[...]


def share_kernel(even_ref, came_ref, mine_ref, *out_refs):
    total = even_ref[...].astype(F32) + came_ref[...].astype(F32)
    mine_ref[...] = total[:PAIR]
    for at, out_ref in enumerate(out_refs):
        out_ref[...] = total[(at + 1) * PAIR : (at + 2) * PAIR].astype(BF16)


def local_kernel(first, q_ref, k_ref, v_ref, g_ref, w_ref, da_ref, s_ref, dp_ref):
    rows = q_ref.shape[0]
    heads = da_ref.shape[1] // HEAD_DIM
    causal = lax.broadcasted_iota(jnp.int32, (rows, rows), 0) <= lax.broadcasted_iota(
        jnp.int32, (rows, rows), 1
    )
    start = first * HEAD_DIM
    turned = dot(w_ref[start : start + heads * HEAD_DIM, :], g_ref[...], NT).astype(BF16)
    da_ref[...] = turned.T
    for head in range(heads):
        cols = head_cols(first + head)
        s_loc = dot(k_ref[:, cols], q_ref[:, cols], NT) * SCALE
        s_ref[head] = jnp.where(causal, s_loc, -jnp.inf)
        dp_ref[head] = dot(v_ref[:, cols], turned[head_cols(head)], NN)


def head_cols(head):
    return slice(head * HEAD_DIM, (head + 1) * HEAD_DIM)


def of_head(refs, head):
    each = refs[0].shape[0]
    return refs[head // each][head % each]


def part_cols(refs, head):
    each = refs[0].shape[1] // HEAD_DIM
    return refs[head // each][:, head_cols(head % each)]


def stacked(refs, cols):
    return jnp.concatenate([ref[:, cols] for ref in refs], axis=0)


def seen(place, slots, rows):
    block = lax.broadcasted_iota(jnp.int32, (slots, rows), 0) // SUMMARY
    half = slots // SUMMARY // 2
    mask = jnp.where(block < half, 2 * block, 2 * (block - half) + 1)
    return (mask ^ place) < place


def attend_kernel(parts, q_ref, v_ref, *rest):
    *ins, attn_ref, p_ref, ds_ref, even_ref, odd_ref, sum_ref = rest
    s_refs, dp_refs, da_refs = ins[:parts], ins[parts : 2 * parts], ins[2 * parts : 3 * parts]
    pieces = ins[3 * parts :]
    place = lax.axis_index("ctx")
    rows = q_ref.shape[0]
    heads = q_ref.shape[1] // HEAD_DIM
    half = even_ref.shape[0]
    blocks = 2 * half // PAIR
    slots = blocks * SUMMARY
    visible = seen(place, slots, rows)
    empty = jnp.zeros((blocks, SUMMARY, rows), F32)
    for head in range(heads):
        cols = head_cols(head)
        both = stacked(pieces, cols)
        s_sum = dot(both, q_ref[:, cols], NT).reshape(blocks, PAIR, rows)
        dp_sum = dot(both, part_cols(da_refs, head), NT).reshape(blocks, PAIR, rows)
        sum_ref[head, 0] = s_sum[:, :SUMMARY].reshape(slots, rows)
        sum_ref[head, 1] = dp_sum[:, SUMMARY:].reshape(slots, rows)
    for head in range(heads):
        s_loc = of_head(s_refs, head)
        s_sum = jnp.where(visible, sum_ref[head, 0] * SCALE, -jnp.inf)
        top = jnp.maximum(
            jnp.max(s_loc, axis=0, keepdims=True), jnp.max(s_sum, axis=0, keepdims=True)
        )
        e_loc = jnp.exp(s_loc - top)
        e_sum = jnp.exp(s_sum - top)
        total = jnp.sum(e_loc, axis=0, keepdims=True) + jnp.sum(e_sum, axis=0, keepdims=True)
        share = 1.0 / total
        p_loc = e_loc * share
        p_sum = e_sum * share
        dp_loc = of_head(dp_refs, head)
        dp_sum = sum_ref[head, 1]
        delta = jnp.sum(p_loc * dp_loc, axis=0, keepdims=True) + jnp.sum(
            p_sum * dp_sum, axis=0, keepdims=True
        )
        ds_loc = p_loc * (dp_loc - delta)
        ds_sum = (p_sum * (dp_sum - delta)).reshape(blocks, SUMMARY, rows)
        at_vals = jnp.concatenate([empty, p_sum.reshape(blocks, SUMMARY, rows)], axis=1)
        at_keys = jnp.concatenate([ds_sum, empty], axis=1)
        p_ref[head, :rows, :] = p_loc.astype(BF16)
        p_ref[head, rows:, :] = at_vals.reshape(blocks * PAIR, rows).astype(BF16)
        ds_ref[head, :rows, :] = ds_loc.astype(BF16)
        ds_ref[head, rows:, :] = at_keys.reshape(blocks * PAIR, rows).astype(BF16)
    for head in range(heads):
        cols = head_cols(head)
        term = dot(ds_ref[head, rows:, :], q_ref[:, cols], NN) * SCALE
        term += dot(p_ref[head, rows:, :], part_cols(da_refs, head), NN)
        even_ref[:, cols] = term[:half].astype(BF16)
        odd_ref[:, cols] = term[half:].astype(BF16)
    for head in range(heads):
        cols = head_cols(head)
        values = jnp.concatenate([v_ref[:, cols], stacked(pieces, cols)], axis=0)
        attn_ref[:, cols] = dot(p_ref[head], values, TN).astype(BF16)


def input_grad_kernel(parts, q_ref, k_ref, p_ref, ds_ref, *rest):
    *ins, dq_ref, dk_ref, dv_ref = rest
    da_refs, pieces = ins[:parts], ins[parts:]
    rows = q_ref.shape[0]
    heads = q_ref.shape[1] // HEAD_DIM
    for head in range(heads):
        cols = head_cols(head)
        dk_ref[:, cols] = dot(ds_ref[head, :rows, :], q_ref[:, cols], NN) * SCALE
        dv_ref[:, cols] = dot(p_ref[head, :rows, :], part_cols(da_refs, head), NN)
    for head in range(heads):
        cols = head_cols(head)
        keys = jnp.concatenate([k_ref[:, cols], stacked(pieces, cols)], axis=0)
        dq_ref[:, cols] = (dot(ds_ref[head], keys, TN) * SCALE).astype(BF16)


def project_kernel(mask, attn_ref, w_ref, send_ref, keep_ref):
    width = send_ref.shape[1]
    rank = lax.axis_index("head")
    target = rank ^ mask
    for goal, out_ref in ((target ^ 1, send_ref), (target, keep_ref)):
        start = pl.multiple_of(goal * width, HEAD_DIM)
        out_ref[...] = dot(attn_ref[...], w_ref[:, pl.ds(start, width)], NN).astype(BF16)


def join_kernel(keep_ref, came_ref, out_ref):
    out_ref[...] = (keep_ref[...].astype(F32) + came_ref[...].astype(F32)).astype(BF16)


def attended_kernel(*refs):
    *parts, out_ref = refs
    total = parts[0][...].astype(F32)
    for part in parts[1:]:
        total = total + part[...].astype(F32)
    out_ref[...] = total.astype(BF16)


def final_kernel(index_ref, dk_ref, dv_ref, *rest):
    *terms, gk_ref, gv_ref = rest
    index = index_ref[0]
    total = terms[0][...].astype(F32)
    for term in terms[1:]:
        total = total + term[...].astype(F32)
    gk_ref[...] = dk_ref[...].astype(BF16)
    gv_ref[...] = dv_ref[...].astype(BF16)
    start = pl.multiple_of((index // 2) * PAIR, PAIR)
    upper = index % 2 == 1
    for ref, out_ref, add in (
        (dk_ref, gk_ref, total[:SUMMARY]),
        (dv_ref, gv_ref, total[SUMMARY:]),
    ):
        low = jnp.where(upper, 0.0, add)
        high = jnp.where(upper, add, 0.0)
        part = ref[pl.ds(start, PAIR), :] + jnp.concatenate([low, high], axis=0)
        out_ref[pl.ds(start, PAIR), :] = part.astype(BF16)


def on_device(queries, key_rows, value_rows, summary_index, out_weight, out_grad):
    rows, width = queries.shape
    heads = width // HEAD_DIM
    shards = lax.axis_size("ctx")
    ranks = lax.axis_size("head")
    half = shards // 2 * PAIR
    slots = shards * SUMMARY
    depth = out_weight.shape[1]
    tall = rows + shards * PAIR

    whole = ((rows, width), BF16)
    own, queries, key_rows, value_rows = call(
        pick_kernel,
        [((PAIR, width), BF16), whole, whole, whole],
        summary_index,
        *(pltpu.with_memory_space_constraint(x, pltpu.HBM) for x in (queries, key_rows, value_rows)),
        smem=1, hbm=3, flops=8 * 10**9,
        scratch=[pltpu.SemaphoreType.DMA((3,))],
    )
    evens = [swap(own, "ctx", mask) for mask in range(2, shards, 2)]

    big = 2 * rows * width * depth
    parts = 2 if heads % 2 == 0 else 1
    each = heads // parts
    das, scores, dps = [], [], []
    gates = (queries, out_grad)
    for first in range(0, heads, each):
        da, score, dp = call(
            functools.partial(local_kernel, first),
            [((rows, each * HEAD_DIM), BF16)] + [((each, rows, rows), F32)] * 2,
            gates[0], key_rows, value_rows, gates[1], out_weight,
            flops=3 * big, moved=width * depth,
        )
        das.append(da)
        scores.append(score)
        dps.append(dp)
        if first == 0:
            evens, own, *gates = lax.optimization_barrier((evens, own, *gates))
            (even,) = call(gather_kernel, [((half, width), BF16)], own, *evens)
            odd = swap(even, "ctx", 1)
            even, *gates = lax.optimization_barrier((even, *gates))
    odd, das = lax.optimization_barrier((odd, das))
    pieces = (even, odd)

    small = 2 * heads * tall * rows * HEAD_DIM
    attn, probs, ds, terms_even, terms_odd = call(
        functools.partial(attend_kernel, parts),
        [whole] + [((heads, tall, rows), BF16)] * 2 + [((half, width), BF16)] * 2,
        queries, value_rows, *scores, *dps, *das, *pieces,
        scratch=[pltpu.VMEM((heads, 2, slots, rows), F32)],
        flops=8 * small,
    )
    came_odd = swap(terms_odd, "ctx", 1)

    def project(mask):
        return call(
            functools.partial(project_kernel, mask),
            [((rows, width), BF16), ((rows, width), BF16)],
            attn, out_weight,
            flops=4 * rows * width * width, moved=4 * width * width,
        )

    came = []
    for mask in range(2, ranks, 2):
        send, keep = project(mask)
        (joined,) = call(join_kernel, [((rows, width), BF16)], keep, swap(send, "head", 1))
        came.append(swap(joined, "head", mask))

    mine, *returned = call(
        share_kernel,
        [((PAIR, width), F32)] + [((PAIR, width), BF16)] * (shards // 2 - 1),
        terms_even, came_odd,
        flops=5 * 10**10,
    )
    returned = [mine] + [swap(term, "ctx", 2 * at + 2) for at, term in enumerate(returned)]
    send, keep = project(0)
    came = [keep, swap(send, "head", 1)] + came
    grad_query, dk, dv = call(
        functools.partial(input_grad_kernel, parts),
        [((rows, width), BF16), ((rows, width), F32), ((rows, width), F32)],
        queries, key_rows, probs, ds, *das, *pieces,
        flops=8 * small,
    )
    grad_key, grad_value = call(
        final_kernel, [((rows, width), BF16), ((rows, width), BF16)], summary_index, dk, dv, *returned, smem=1
    )
    (attended,) = call(attended_kernel, [((rows, width), BF16)], *came)
    return (attended, grad_query, grad_key, grad_value)


def solution(mesh):
    return jax.shard_map(
        on_device,
        mesh=mesh,
        in_specs=(
            P("ctx", "head"),
            P("ctx", "head"),
            P("ctx", "head"),
            P("ctx"),
            P("head", None),
            P("ctx", None),
        ),
        out_specs=(P("ctx", "head"), P("ctx", "head"), P("ctx", "head"), P("ctx", "head")),
        check_vma=False,
    )
```

```python
import functools

import jax
import jax.numpy as jnp
from jax import lax
from jax.experimental import pallas as pl
from jax.experimental.pallas import tpu as pltpu
from jax.sharding import PartitionSpec as P

HEAD_DIM = 128
STRIDE = 128
SUMMARY = 8
PAIR = 2 * SUMMARY
SCALE = HEAD_DIM ** (-0.5)
NT = (((1,), (1,)), ((), ()))
NN = (((1,), (0,)), ((), ()))
TN = (((0,), (0,)), ((), ()))
BF16 = jnp.bfloat16
F32 = jnp.float32
VMEM_LIMIT = 12 * 1024 * 1024


def dot(a, b, dims):
    return lax.dot_general(a, b, dims, preferred_element_type=F32)


def call(body, outs, *args, smem=0, hbm=0, hbm_outs=0, alias=None, scratch=(), flops=0, moved=0):
    vmem = pl.BlockSpec(memory_space=pltpu.VMEM)
    far = pl.BlockSpec(memory_space=pl.ANY)
    args = [
        pltpu.with_memory_space_constraint(x, pltpu.HBM) if smem <= at < smem + hbm else x
        for at, x in enumerate(args)
    ]
    shapes = [pltpu.HBM(shape, dtype) for shape, dtype in outs[:hbm_outs]]
    shapes += [jax.ShapeDtypeStruct(shape, dtype) for shape, dtype in outs[hbm_outs:]]
    return pl.pallas_call(
        body,
        in_specs=[pl.BlockSpec(memory_space=pltpu.SMEM)] * smem
        + [far] * hbm
        + [vmem] * (len(args) - smem - hbm),
        out_specs=[far] * hbm_outs + [vmem] * (len(outs) - hbm_outs),
        out_shape=shapes,
        input_output_aliases=alias or {},
        scratch_shapes=scratch,
        compiler_params=pltpu.CompilerParams(vmem_limit_bytes=VMEM_LIMIT),
        cost_estimate=pl.CostEstimate(flops=flops, bytes_accessed=moved, transcendentals=0),
    )(*args)


def swap(value, axis, mask):
    return lax.ppermute(value, axis, [(i, i ^ mask) for i in range(lax.axis_size(axis))])


def slot_rows(index):
    return pl.ds(pl.multiple_of((index // 2) * PAIR, PAIR), PAIR), index % 2 == 1


def pick_kernel(index_ref, q_ref, k_ref, v_ref, own_ref, q_out, k_out, v_out, sems):
    pairs = ((k_ref, k_out), (v_ref, v_out), (q_ref, q_out))
    copies = [
        pltpu.make_async_copy(source, target, sems.at[i]) for i, (source, target) in enumerate(pairs)
    ]
    for copy in copies:
        copy.start()
    for copy in copies[:2]:
        copy.wait()
    there, upper = slot_rows(index_ref[0])
    k = k_out[there, :].astype(F32)
    v = v_out[there, :].astype(F32)
    k = jnp.where(upper, k[SUMMARY:], k[:SUMMARY])
    v = jnp.where(upper, v[SUMMARY:], v[:SUMMARY])
    own_ref[...] = jnp.concatenate([k, v], axis=0).astype(BF16)
    copies[2].wait()


def gather_kernel(*refs):
    *parts, out_ref = refs
    for at, part in enumerate(parts):
        out_ref[at * PAIR : (at + 1) * PAIR, :] = part[...]


def share_kernel(first, even_ref, came_ref, *out_refs):
    count = came_ref.shape[0]
    total = even_ref[first : first + count, :].astype(F32) + came_ref[...].astype(F32)
    for at, out_ref in enumerate(out_refs):
        out_ref[...] = total[at * PAIR : (at + 1) * PAIR].astype(out_ref.dtype)


def local_kernel(first, q_ref, k_ref, v_ref, g_ref, w_ref, da_ref, s_ref, dp_ref):
    rows = q_ref.shape[0]
    heads = da_ref.shape[1] // HEAD_DIM
    causal = lax.broadcasted_iota(jnp.int32, (rows, rows), 0) <= lax.broadcasted_iota(
        jnp.int32, (rows, rows), 1
    )
    start = first * HEAD_DIM
    turned = dot(w_ref[start : start + heads * HEAD_DIM, :], g_ref[...], NT).astype(BF16)
    da_ref[...] = turned.T
    for head in range(heads):
        cols = head_cols(first + head)
        s_loc = dot(k_ref[:, cols], q_ref[:, cols], NT) * SCALE
        s_ref[head] = jnp.where(causal, s_loc, -jnp.inf)
        dp_ref[head] = dot(v_ref[:, cols], turned[head_cols(head)], NN)


def head_cols(head):
    return slice(head * HEAD_DIM, (head + 1) * HEAD_DIM)


def of_head(refs, head):
    for ref in refs:
        if head < ref.shape[0]:
            return ref[head]
        head -= ref.shape[0]


def part_cols(refs, head):
    for ref in refs:
        if head < ref.shape[1] // HEAD_DIM:
            return ref[:, head_cols(head)]
        head -= ref.shape[1] // HEAD_DIM


def stacked(refs, cols):
    return jnp.concatenate([ref[:, cols] for ref in refs], axis=0)


def seen(place, slots, rows):
    block = lax.broadcasted_iota(jnp.int32, (slots, rows), 0) // SUMMARY
    half = slots // SUMMARY // 2
    mask = jnp.where(block < half, 2 * block, 2 * (block - half) + 1)
    return (mask ^ place) < place


def attend_kernel(parts, q_ref, v_ref, *rest):
    *ins, attn_ref, p_ref, ds_ref, even_ref, near_ref, far_ref, sum_ref = rest
    s_refs, dp_refs, da_refs = ins[:parts], ins[parts : 2 * parts], ins[2 * parts : 3 * parts]
    pieces = ins[3 * parts :]
    place = lax.axis_index("ctx")
    rows = q_ref.shape[0]
    heads = q_ref.shape[1] // HEAD_DIM
    half = even_ref.shape[0]
    blocks = 2 * half // PAIR
    slots = blocks * SUMMARY
    visible = seen(place, slots, rows)
    empty = jnp.zeros((blocks, SUMMARY, rows), F32)
    for head in range(heads):
        cols = head_cols(head)
        both = stacked(pieces, cols)
        s_sum = dot(both, q_ref[:, cols], NT).reshape(blocks, PAIR, rows)
        dp_sum = dot(both, part_cols(da_refs, head), NT).reshape(blocks, PAIR, rows)
        sum_ref[head, 0] = s_sum[:, :SUMMARY].reshape(slots, rows)
        sum_ref[head, 1] = dp_sum[:, SUMMARY:].reshape(slots, rows)
    for head in range(heads):
        s_loc = of_head(s_refs, head)
        s_sum = jnp.where(visible, sum_ref[head, 0] * SCALE, -jnp.inf)
        top = jnp.maximum(
            jnp.max(s_loc, axis=0, keepdims=True), jnp.max(s_sum, axis=0, keepdims=True)
        )
        e_loc = jnp.exp(s_loc - top)
        e_sum = jnp.exp(s_sum - top)
        total = jnp.sum(e_loc, axis=0, keepdims=True) + jnp.sum(e_sum, axis=0, keepdims=True)
        share = 1.0 / total
        p_loc = e_loc * share
        p_sum = e_sum * share
        dp_loc = of_head(dp_refs, head)
        dp_sum = sum_ref[head, 1]
        delta = jnp.sum(p_loc * dp_loc, axis=0, keepdims=True) + jnp.sum(
            p_sum * dp_sum, axis=0, keepdims=True
        )
        ds_loc = p_loc * (dp_loc - delta)
        ds_sum = (p_sum * (dp_sum - delta)).reshape(blocks, SUMMARY, rows)
        at_vals = jnp.concatenate([empty, p_sum.reshape(blocks, SUMMARY, rows)], axis=1)
        at_keys = jnp.concatenate([ds_sum, empty], axis=1)
        p_ref[head, :rows, :] = p_loc.astype(BF16)
        p_ref[head, rows:, :] = at_vals.reshape(blocks * PAIR, rows).astype(BF16)
        ds_ref[head, :rows, :] = ds_loc.astype(BF16)
        ds_ref[head, rows:, :] = at_keys.reshape(blocks * PAIR, rows).astype(BF16)
    for head in range(heads):
        cols = head_cols(head)
        term = dot(ds_ref[head, rows:, :], q_ref[:, cols], NN) * SCALE
        term += dot(p_ref[head, rows:, :], part_cols(da_refs, head), NN)
        even_ref[:, cols] = term[:half].astype(BF16)
        near_ref[:, cols] = term[half : half + half // 2].astype(BF16)
        far_ref[:, cols] = term[half + half // 2 :].astype(BF16)
    for head in range(heads):
        cols = head_cols(head)
        values = jnp.concatenate([v_ref[:, cols], stacked(pieces, cols)], axis=0)
        attn_ref[:, cols] = dot(p_ref[head], values, TN).astype(BF16)


def input_grad_kernel(parts, index_ref, q_ref, k_ref, p_ref, ds_ref, *rest):
    *ins, gk_out, gv_out, dq_ref, k_rows, v_rows, dk_ref, dv_ref, gk_ref, gv_ref, sems = rest
    da_refs, pieces = ins[:parts], ins[parts:]
    heads = q_ref.shape[1] // HEAD_DIM
    rows = q_ref.shape[0]
    for head in range(heads):
        cols = head_cols(head)
        dk_ref[:, cols] = dot(ds_ref[head, :rows, :], q_ref[:, cols], NN) * SCALE
        dv_ref[:, cols] = dot(p_ref[head, :rows, :], part_cols(da_refs, head), NN)
    gk_ref[...] = dk_ref[...].astype(BF16)
    gv_ref[...] = dv_ref[...].astype(BF16)
    stores = [
        pltpu.make_async_copy(gk_ref, gk_out, sems.at[1]),
        pltpu.make_async_copy(gv_ref, gv_out, sems.at[2]),
    ]
    for store in stores:
        store.start()
    for head in range(heads):
        cols = head_cols(head)
        keys = jnp.concatenate([k_ref[:, cols], stacked(pieces, cols)], axis=0)
        dq_ref[:, cols] = (dot(ds_ref[head], keys, TN) * SCALE).astype(BF16)
    there, upper = slot_rows(index_ref[0])
    k_rows[...] = dk_ref[there, :]
    v_rows[...] = dv_ref[there, :]
    for store in stores:
        store.wait()


def project_kernel(mask, attn_ref, w_ref, send_ref, keep_ref):
    width = send_ref.shape[1]
    rank = lax.axis_index("head")
    target = rank ^ mask
    for goal, out_ref in ((target ^ 1, send_ref), (target, keep_ref)):
        start = pl.multiple_of(goal * width, HEAD_DIM)
        out_ref[...] = dot(attn_ref[...], w_ref[:, pl.ds(start, width)], NN).astype(BF16)


def join_kernel(keep_ref, came_ref, out_ref):
    out_ref[...] = (keep_ref[...].astype(F32) + came_ref[...].astype(F32)).astype(BF16)


def final_kernel(terms, index_ref, gk_ref, gv_ref, k_rows, v_rows, *rest):
    *ins, gk_out, gv_out, out_ref, k_new, v_new, sems = rest
    terms, sums = ins[:terms], ins[terms:]
    total = terms[0][...].astype(F32)
    for term in terms[1:]:
        total = total + term[...].astype(F32)
    there, upper = slot_rows(index_ref[0])
    stores = []
    for at, (rows, add, new, out) in enumerate(
        ((k_rows, total[:SUMMARY], k_new, gk_out), (v_rows, total[SUMMARY:], v_new, gv_out))
    ):
        low = jnp.where(upper, 0.0, add)
        high = jnp.where(upper, add, 0.0)
        new[...] = (rows[...] + jnp.concatenate([low, high], axis=0)).astype(BF16)
        stores.append(pltpu.make_async_copy(new, out.at[there, :], sems.at[1 + at]))
        stores[-1].start()
    total = sums[0][...].astype(F32)
    for part in sums[1:]:
        total = total + part[...].astype(F32)
    out_ref[...] = total.astype(BF16)
    for store in stores:
        store.wait()


def on_device(queries, key_rows, value_rows, summary_index, out_weight, out_grad):
    rows, width = queries.shape
    heads = width // HEAD_DIM
    shards = lax.axis_size("ctx")
    ranks = lax.axis_size("head")
    half = shards // 2 * PAIR
    slots = shards * SUMMARY
    depth = out_weight.shape[1]
    tall = rows + shards * PAIR

    whole = ((rows, width), BF16)
    own, queries, key_rows, value_rows = call(
        pick_kernel,
        [((PAIR, width), BF16), whole, whole, whole],
        summary_index, queries, key_rows, value_rows,
        smem=1, hbm=3, flops=8 * 10**9,
        scratch=[pltpu.SemaphoreType.DMA((4,))],
    )
    evens = [swap(own, "ctx", mask) for mask in range(2, shards, 2)]
    beside = swap(own, "ctx", 1)

    big = 2 * rows * width * depth
    das, scores, dps = [], [], []
    gates = (queries, out_grad)
    first = 0
    for count in (max(heads // 3, 1), heads - max(heads // 3, 1)):
        da, score, dp = call(
            functools.partial(local_kernel, first),
            [((rows, count * HEAD_DIM), BF16)] + [((count, rows, rows), F32)] * 2,
            gates[0], key_rows, value_rows, gates[1], out_weight,
            flops=3 * big, moved=width * depth,
        )
        das.append(da)
        scores.append(score)
        dps.append(dp)
        if first == 0:
            evens, *gates = lax.optimization_barrier((evens, *gates))
            (even,) = call(gather_kernel, [((half - PAIR, width), BF16)], *evens)
            odd = swap(even, "ctx", 1)
            even, *gates = lax.optimization_barrier((even, *gates))
        first += count
    beside, odd, das = lax.optimization_barrier((beside, odd, das))
    pieces = (own, even, beside, odd)
    parts = len(das)

    small = 2 * heads * tall * rows * HEAD_DIM
    attn, probs, ds, terms, near, far = call(
        functools.partial(attend_kernel, parts),
        [whole] + [((heads, tall, rows), BF16)] * 2
        + [((half, width), BF16)] + [((half // 2, width), BF16)] * 2,
        queries, value_rows, *scores, *dps, *das, *pieces,
        scratch=[pltpu.VMEM((heads, 2, slots, rows), F32)],
        flops=8 * small,
    )
    far = swap(far, "ctx", 1)
    near = swap(near, "ctx", 1)

    def project(mask, attn):
        return call(
            functools.partial(project_kernel, mask),
            [((rows, width), BF16), ((rows, width), BF16)],
            attn, out_weight,
            flops=1, moved=1,
        )

    came = []
    for mask in range(2, ranks, 2):
        send, keep = project(mask, attn)
        (joined,) = call(join_kernel, [whole], keep, swap(send, "head", 1))
        came.append(swap(joined, "head", mask))
        joined, attn = lax.optimization_barrier((joined, attn))

    block = ((PAIR, width), BF16)
    quarter = shards // 4
    returned = call(
        functools.partial(share_kernel, half // 2), [block] * quarter, terms, far, flops=5 * 10**10
    )
    mine, *closer = call(
        functools.partial(share_kernel, 0),
        [((PAIR, width), F32)] + [block] * (quarter - 1),
        terms, near,
        flops=10**10,
    )
    returned = [mine] + [swap(term, "ctx", 2 * (quarter + at)) for at, term in enumerate(returned)]
    returned += [swap(term, "ctx", 2 * at + 2) for at, term in enumerate(closer)]
    send, keep = project(0, attn)
    came = [keep, swap(send, "head", 1)] + came
    wide = pltpu.VMEM((rows, width), F32)
    slim = pltpu.VMEM((rows, width), BF16)
    grad_key, grad_value, grad_query, k_rows, v_rows = call(
        functools.partial(input_grad_kernel, parts),
        [whole, whole, whole, ((PAIR, width), F32), ((PAIR, width), F32)],
        summary_index, queries, key_rows, probs, ds, *das, *pieces,
        smem=1, hbm_outs=2, flops=8 * small,
        scratch=[wide, wide, slim, slim, pltpu.SemaphoreType.DMA((3,))],
    )
    patch = pltpu.VMEM((PAIR, width), BF16)
    grad_key, grad_value, attended = call(
        functools.partial(final_kernel, len(returned)),
        [whole, whole, whole],
        summary_index, grad_key, grad_value, k_rows, v_rows, *returned, *came,
        smem=1, hbm=2, hbm_outs=2, alias={1: 0, 2: 1},
        scratch=[patch, patch, pltpu.SemaphoreType.DMA((3,))],
    )
    return (attended, grad_query, grad_key, grad_value)


def solution(mesh):
    return jax.shard_map(
        on_device,
        mesh=mesh,
        in_specs=(
            P("ctx", "head"),
            P("ctx", "head"),
            P("ctx", "head"),
            P("ctx"),
            P("head", None),
            P("ctx", None),
        ),
        out_specs=(P("ctx", "head"), P("ctx", "head"), P("ctx", "head"), P("ctx", "head")),
        check_vma=False,
    )
```

```python
import functools

import jax
import jax.numpy as jnp
from jax import lax
from jax.experimental import pallas as pl
from jax.experimental.pallas import tpu as pltpu
from jax.sharding import PartitionSpec as P

HEAD_DIM = 128
STRIDE = 128
SUMMARY = 8
PAIR = 2 * SUMMARY
FINAL_PARTS = 3
SCALE = HEAD_DIM ** (-0.5)
NT = (((1,), (1,)), ((), ()))
NN = (((1,), (0,)), ((), ()))
TN = (((0,), (0,)), ((), ()))
BF16 = jnp.bfloat16
F32 = jnp.float32
VMEM_LIMIT = 12 * 1024 * 1024


def dot(a, b, dims):
    return lax.dot_general(a, b, dims, preferred_element_type=F32)


def call(
    body, outs, *args, smem=0, hbm=0, hbm_outs=0, alias=None, scratch=(), flops=0, moved=0, after=()
):
    vmem = pl.BlockSpec(memory_space=pltpu.VMEM)
    far = pl.BlockSpec(memory_space=pl.ANY)
    args = [
        pltpu.with_memory_space_constraint(x, pltpu.HBM) if smem <= at < smem + hbm else x
        for at, x in enumerate(args)
    ]
    shapes = [pltpu.HBM(shape, dtype) for shape, dtype in outs[:hbm_outs]]
    shapes += [jax.ShapeDtypeStruct(shape, dtype) for shape, dtype in outs[hbm_outs:]]
    plain = len(args)

    def ordered(*refs):
        body(*refs[:plain], *refs[plain + len(after) :])

    return pl.pallas_call(
        ordered,
        in_specs=[pl.BlockSpec(memory_space=pltpu.SMEM)] * smem
        + [far] * hbm
        + [vmem] * (plain - smem - hbm)
        + [far] * len(after),
        out_specs=[far] * hbm_outs + [vmem] * (len(outs) - hbm_outs),
        out_shape=shapes,
        input_output_aliases=alias or {},
        scratch_shapes=scratch,
        compiler_params=pltpu.CompilerParams(vmem_limit_bytes=VMEM_LIMIT),
        cost_estimate=pl.CostEstimate(flops=flops, bytes_accessed=moved, transcendentals=0),
    )(*args, *after)


def swap(value, axis, mask):
    return lax.ppermute(value, axis, [(i, i ^ mask) for i in range(lax.axis_size(axis))])


def slot_rows(index):
    return pl.ds(pl.multiple_of((index // 2) * PAIR, PAIR), PAIR), index % 2 == 1


def pick_kernel(index_ref, k_ref, v_ref, own_ref, k_rows, v_rows, sems):
    there, upper = slot_rows(index_ref[0])
    copies = [
        pltpu.make_async_copy(k_ref.at[there, :], k_rows, sems.at[0]),
        pltpu.make_async_copy(v_ref.at[there, :], v_rows, sems.at[1]),
    ]
    for copy in copies:
        copy.start()
    for copy in copies:
        copy.wait()
    k = k_rows[...].astype(F32)
    v = v_rows[...].astype(F32)
    k = jnp.where(upper, k[SUMMARY:], k[:SUMMARY])
    v = jnp.where(upper, v[SUMMARY:], v[:SUMMARY])
    own_ref[...] = jnp.concatenate([k, v], axis=0).astype(BF16)


def gather_kernel(*refs):
    *parts, out_ref = refs
    for at, part in enumerate(parts):
        out_ref[at * PAIR : (at + 1) * PAIR, :] = part[...]


def share_kernel(even_ref, came_ref, carried_in, carried_out, *out_refs):
    for at, out_ref in enumerate(out_refs):
        mine = even_ref[(at + 1) * PAIR : (at + 2) * PAIR, :].astype(F32)
        came = came_ref[at * PAIR : (at + 1) * PAIR, :].astype(F32)
        out_ref[...] = (mine + came).astype(BF16)


def local_kernel(first, q_ref, k_ref, v_ref, g_ref, w_ref, da_ref, s_ref, dp_ref):
    rows = g_ref.shape[0]
    heads = da_ref.shape[1] // HEAD_DIM
    causal = lax.broadcasted_iota(jnp.int32, (rows, rows), 0) <= lax.broadcasted_iota(
        jnp.int32, (rows, rows), 1
    )
    start = first * HEAD_DIM
    turned = dot(w_ref[start : start + heads * HEAD_DIM, :], g_ref[...], NT).astype(BF16)
    da_ref[...] = turned.T
    for head in range(heads):
        cols = head_cols(first + head)
        s_loc = dot(k_ref[:, cols], q_ref[:, cols], NT) * SCALE
        s_ref[head] = jnp.where(causal, s_loc, -jnp.inf)
        dp_ref[head] = dot(v_ref[:, cols], turned[head_cols(head)], NN)


def head_cols(head):
    return slice(head * HEAD_DIM, (head + 1) * HEAD_DIM)


def of_head(refs, head):
    for ref in refs:
        if head < ref.shape[0]:
            return ref[head]
        head -= ref.shape[0]


def part_cols(refs, head):
    for ref in refs:
        if head < ref.shape[1] // HEAD_DIM:
            return ref[:, head_cols(head)]
        head -= ref.shape[1] // HEAD_DIM


def stacked(refs, cols):
    return jnp.concatenate([ref[:, cols] for ref in refs], axis=0)


def seen(place, slots, rows):
    block = lax.broadcasted_iota(jnp.int32, (slots, rows), 0) // SUMMARY
    half = slots // SUMMARY // 2
    mask = jnp.where(block < half, 2 * block, 2 * (block - half) + 1)
    return (mask ^ place) < place


def attend_kernel(parts, q_ref, v_ref, *rest):
    *ins, attn_ref, p_ref, ds_ref, even_ref, next_ref, odd_ref, sum_ref = rest
    s_refs, dp_refs, da_refs = ins[:parts], ins[parts : 2 * parts], ins[2 * parts : 3 * parts]
    pieces = ins[3 * parts :]
    place = lax.axis_index("ctx")
    rows = q_ref.shape[0]
    heads = q_ref.shape[1] // HEAD_DIM
    half = even_ref.shape[0]
    blocks = 2 * half // PAIR
    slots = blocks * SUMMARY
    visible = seen(place, slots, rows)
    empty = jnp.zeros((blocks, SUMMARY, rows), F32)
    for head in range(heads):
        cols = head_cols(head)
        both = stacked(pieces, cols)
        s_sum = dot(both, q_ref[:, cols], NT).reshape(blocks, PAIR, rows)
        dp_sum = dot(both, part_cols(da_refs, head), NT).reshape(blocks, PAIR, rows)
        sum_ref[head, 0] = s_sum[:, :SUMMARY].reshape(slots, rows)
        sum_ref[head, 1] = dp_sum[:, SUMMARY:].reshape(slots, rows)
    for head in range(heads):
        s_loc = of_head(s_refs, head)
        s_sum = jnp.where(visible, sum_ref[head, 0] * SCALE, -jnp.inf)
        top = jnp.maximum(
            jnp.max(s_loc, axis=0, keepdims=True), jnp.max(s_sum, axis=0, keepdims=True)
        )
        e_loc = jnp.exp(s_loc - top)
        e_sum = jnp.exp(s_sum - top)
        total = jnp.sum(e_loc, axis=0, keepdims=True) + jnp.sum(e_sum, axis=0, keepdims=True)
        share = 1.0 / total
        p_loc = e_loc * share
        p_sum = e_sum * share
        dp_loc = of_head(dp_refs, head)
        dp_sum = sum_ref[head, 1]
        delta = jnp.sum(p_loc * dp_loc, axis=0, keepdims=True) + jnp.sum(
            p_sum * dp_sum, axis=0, keepdims=True
        )
        ds_loc = p_loc * (dp_loc - delta)
        ds_sum = (p_sum * (dp_sum - delta)).reshape(blocks, SUMMARY, rows)
        at_vals = jnp.concatenate([empty, p_sum.reshape(blocks, SUMMARY, rows)], axis=1)
        at_keys = jnp.concatenate([ds_sum, empty], axis=1)
        p_ref[head, :rows, :] = p_loc.astype(BF16)
        p_ref[head, rows:, :] = at_vals.reshape(blocks * PAIR, rows).astype(BF16)
        ds_ref[head, :rows, :] = ds_loc.astype(BF16)
        ds_ref[head, rows:, :] = at_keys.reshape(blocks * PAIR, rows).astype(BF16)
    for head in range(heads):
        cols = head_cols(head)
        term = dot(ds_ref[head, rows:, :], q_ref[:, cols], NN) * SCALE
        term += dot(p_ref[head, rows:, :], part_cols(da_refs, head), NN)
        even_ref[:, cols] = term[:half].astype(BF16)
        next_ref[:, cols] = term[half : half + PAIR].astype(BF16)
        odd_ref[:, cols] = term[half + PAIR :].astype(BF16)
    for head in range(heads):
        cols = head_cols(head)
        values = jnp.concatenate([v_ref[:, cols], stacked(pieces, cols)], axis=0)
        attn_ref[:, cols] = dot(p_ref[head], values, TN).astype(BF16)


def input_grad_kernel(parts, index_ref, q_ref, k_ref, p_ref, ds_ref, *rest):
    *ins, gk_out, gv_out, dq_ref, k_rows, v_rows, dk_ref, dv_ref, gk_ref, gv_ref, sems = rest
    da_refs, pieces = ins[:parts], ins[parts:]
    heads = q_ref.shape[1] // HEAD_DIM
    rows = q_ref.shape[0]
    for head in range(heads):
        cols = head_cols(head)
        dk_ref[:, cols] = dot(ds_ref[head, :rows, :], q_ref[:, cols], NN) * SCALE
        dv_ref[:, cols] = dot(p_ref[head, :rows, :], part_cols(da_refs, head), NN)
    gk_ref[...] = dk_ref[...].astype(BF16)
    gv_ref[...] = dv_ref[...].astype(BF16)
    stores = [
        pltpu.make_async_copy(gk_ref, gk_out, sems.at[1]),
        pltpu.make_async_copy(gv_ref, gv_out, sems.at[2]),
    ]
    for store in stores:
        store.start()
    for head in range(heads):
        cols = head_cols(head)
        keys = jnp.concatenate([k_ref[:, cols], stacked(pieces, cols)], axis=0)
        dq_ref[:, cols] = (dot(ds_ref[head], keys, TN) * SCALE).astype(BF16)
    there, upper = slot_rows(index_ref[0])
    k_rows[...] = dk_ref[there, :]
    v_rows[...] = dv_ref[there, :]
    for store in stores:
        store.wait()


def project_kernel(mask, attn_ref, w_ref, *out_refs):
    width = attn_ref.shape[1]
    start = pl.multiple_of((lax.axis_index("head") ^ mask) * width, HEAD_DIM)
    out = dot(attn_ref[...], w_ref[:, pl.ds(start, width)], NN).astype(BF16)
    each = width // len(out_refs)
    for at, out_ref in enumerate(out_refs):
        out_ref[...] = out[:, at * each : (at + 1) * each]


def join_kernel(keep_ref, *rest):
    *came_refs, out_ref = rest
    each = came_refs[0].shape[1]
    for at, came_ref in enumerate(came_refs):
        cols = slice(at * each, (at + 1) * each)
        out_ref[:, cols] = (keep_ref[:, cols].astype(F32) + came_ref[...].astype(F32)).astype(BF16)


def final_kernel(terms, index_ref, gk_ref, gv_ref, k_rows, v_rows, *rest):
    *ins, gk_out, gv_out, out, k_new, v_new, held, sems = rest
    terms, sums = ins[:terms], ins[terms:]
    there, upper = slot_rows(index_ref[0])
    width = held.shape[1]
    step = width // FINAL_PARTS
    stores = []
    for at in range(FINAL_PARTS):
        cols = slice(at * step, (at + 1) * step)
        total = sums[0][:, cols].astype(F32)
        for part in sums[1:]:
            total = total + part[:, cols].astype(F32)
        held[:, cols] = total.astype(BF16)
        stores.append(pltpu.make_async_copy(held.at[:, cols], out.at[:, cols], sems.at[2 + at]))
        stores[-1].start()
    total = terms[0][:PAIR, :].astype(F32)
    for term in terms[1:]:
        total = total + term[...].astype(F32)
    for at, (rows, add, new, target) in enumerate(
        ((k_rows, total[:SUMMARY], k_new, gk_out), (v_rows, total[SUMMARY:], v_new, gv_out))
    ):
        low = jnp.where(upper, 0.0, add)
        high = jnp.where(upper, add, 0.0)
        new[...] = (rows[...] + jnp.concatenate([low, high], axis=0)).astype(BF16)
        stores.append(pltpu.make_async_copy(new, target.at[there, :], sems.at[at]))
        stores[-1].start()
    for store in stores:
        store.wait()


def on_device(queries, key_rows, value_rows, summary_index, out_weight, out_grad):
    rows, width = queries.shape
    heads = width // HEAD_DIM
    shards = lax.axis_size("ctx")
    ranks = lax.axis_size("head")
    half = shards // 2 * PAIR
    slots = shards * SUMMARY
    depth = out_weight.shape[1]
    tall = rows + shards * PAIR

    whole = ((rows, width), BF16)
    rows_held = pltpu.VMEM((PAIR, width), BF16)
    (own,) = call(
        pick_kernel,
        [((PAIR, width), BF16)],
        summary_index, key_rows, value_rows,
        smem=1, hbm=2, flops=8 * 10**9,
        scratch=[rows_held, rows_held, pltpu.SemaphoreType.DMA((2,))],
    )
    evens = [swap(own, "ctx", mask) for mask in range(2, shards, 2)]

    def local(first, count):
        return call(
            functools.partial(local_kernel, first),
            [((rows, count * HEAD_DIM), BF16)]
            + [((count, rows, rows), F32)] * 2,
            queries, key_rows, value_rows, out_grad, out_weight,
            flops=6 * rows * width * depth, moved=width * depth,
        )

    def across(blocks, after):
        (joint,) = call(
            gather_kernel, [((len(blocks) * PAIR, width), BF16)], *blocks, flops=1, moved=1, after=after
        )
        return [joint, swap(joint, "ctx", 1)]

    das, scores, dps, pieces = [], [], [], []
    ends = [max(heads // 3, 1), heads]
    first = 0
    for turn, end in enumerate(ends):
        da, score, dp = local(first, end - first)
        das.append(da)
        scores.append(score)
        dps.append(dp)
        first = end
        if turn == 0:
            pieces = [own, across(evens, (da,))]
    beside = swap(own, "ctx", 1)
    pieces = [own, pieces[1][0], beside, pieces[1][1]]
    parts = len(das)

    small = 2 * heads * tall * rows * HEAD_DIM
    attn, probs, ds, terms, beside, odds = call(
        functools.partial(attend_kernel, parts),
        [whole] + [((heads, tall, rows), BF16)] * 2
        + [((half, width), BF16), ((PAIR, width), BF16), ((half - PAIR, width), BF16)],
        queries, value_rows, *scores, *dps, *das, *pieces,
        scratch=[pltpu.VMEM((heads, 2, slots, rows), F32)],
        flops=8 * small,
    )

    def project(mask, cuts=1, after=()):
        cuts = cuts if width % (cuts * HEAD_DIM) == 0 else 1
        return call(
            functools.partial(project_kernel, mask),
            [((rows, width // cuts), BF16)] * cuts,
            attn, out_weight,
            flops=1, moved=1, after=after,
        )

    def exchanged(mask, cuts):
        sends = [swap(send, "head", 1) for send in project(mask ^ 1, cuts)]
        return [*project(mask), *sends]

    came = []
    for mask in range(2, ranks, 2):
        keep, *sends = exchanged(mask, 3)
        (joined,) = call(join_kernel, [whole], keep, *sends)
        came.append(swap(joined, "head", mask))

    beside, *returned = call(
        share_kernel,
        [((PAIR, width), BF16)] * (shards // 2),
        terms, swap(odds, "ctx", 1), beside,
        alias={2: 0},
        flops=5 * 10**10, after=(),
    )
    returned = [swap(term, "ctx", 2 * at + 2) for at, term in enumerate(returned)]
    returned.append(swap(beside, "ctx", 1))
    sends = [swap(send, "head", 1) for send in project(1)]
    came = [*project(0, after=(returned[0],)), *sends, *came]
    wide = pltpu.VMEM((rows, width), F32)
    slim = pltpu.VMEM((rows, width), BF16)
    grad_key, grad_value, grad_query, k_rows, v_rows = call(
        functools.partial(input_grad_kernel, parts),
        [whole, whole, whole, ((PAIR, width), F32), ((PAIR, width), F32)],
        summary_index, queries, key_rows, probs, ds, *das, *pieces,
        smem=1, hbm_outs=2, flops=8 * small, after=(),
        scratch=[wide, wide, slim, slim, pltpu.SemaphoreType.DMA((3,))],
    )
    patch = pltpu.VMEM((PAIR, width), BF16)
    grad_key, grad_value, attended = call(
        functools.partial(final_kernel, 1 + len(returned)),
        [whole, whole, whole],
        summary_index, grad_key, grad_value, k_rows, v_rows, terms, *returned, *came,
        smem=1, hbm=2, hbm_outs=3, alias={1: 0, 2: 1},
        scratch=[patch, patch, slim, pltpu.SemaphoreType.DMA((2 + FINAL_PARTS,))],
    )
    return (attended, grad_query, grad_key, grad_value)


def solution(mesh):
    return jax.shard_map(
        on_device,
        mesh=mesh,
        in_specs=(
            P("ctx", "head"),
            P("ctx", "head"),
            P("ctx", "head"),
            P("ctx"),
            P("head", None),
            P("ctx", None),
        ),
        out_specs=(P("ctx", "head"), P("ctx", "head"), P("ctx", "head"), P("ctx", "head")),
        check_vma=False,
    )
```

```python
import functools

import jax
import jax.numpy as jnp
from jax import lax
from jax.experimental import pallas as pl
from jax.experimental.pallas import tpu as pltpu
from jax.sharding import PartitionSpec as P

HEAD_DIM = 128
STRIDE = 128
SUMMARY = 8
PAIR = 2 * SUMMARY
FINAL_PARTS = 3
SCALE = HEAD_DIM ** (-0.5)
NT = (((1,), (1,)), ((), ()))
NN = (((1,), (0,)), ((), ()))
TN = (((0,), (0,)), ((), ()))
BF16 = jnp.bfloat16
F32 = jnp.float32
VMEM_LIMIT = 12 * 1024 * 1024


def dot(a, b, dims):
    return lax.dot_general(a, b, dims, preferred_element_type=F32)


def call(
    body, outs, *args, smem=0, hbm=0, hbm_outs=0, alias=None, scratch=(), flops=0, moved=0, after=()
):
    vmem = pl.BlockSpec(memory_space=pltpu.VMEM)
    far = pl.BlockSpec(memory_space=pl.ANY)
    args = [
        pltpu.with_memory_space_constraint(x, pltpu.HBM) if smem <= at < smem + hbm else x
        for at, x in enumerate(args)
    ]
    shapes = [pltpu.HBM(shape, dtype) for shape, dtype in outs[:hbm_outs]]
    shapes += [jax.ShapeDtypeStruct(shape, dtype) for shape, dtype in outs[hbm_outs:]]
    plain = len(args)

    def ordered(*refs):
        body(*refs[:plain], *refs[plain + len(after) :])

    return pl.pallas_call(
        ordered,
        in_specs=[pl.BlockSpec(memory_space=pltpu.SMEM)] * smem
        + [far] * hbm
        + [vmem] * (plain - smem - hbm)
        + [far] * len(after),
        out_specs=[far] * hbm_outs + [vmem] * (len(outs) - hbm_outs),
        out_shape=shapes,
        input_output_aliases=alias or {},
        scratch_shapes=scratch,
        compiler_params=pltpu.CompilerParams(vmem_limit_bytes=VMEM_LIMIT),
        cost_estimate=pl.CostEstimate(flops=flops, bytes_accessed=moved, transcendentals=0),
    )(*args, *after)


def swap(value, axis, mask):
    return lax.ppermute(value, axis, [(i, i ^ mask) for i in range(lax.axis_size(axis))])


def slot_rows(index):
    return pl.ds(pl.multiple_of((index // 2) * PAIR, PAIR), PAIR), index % 2 == 1


def pick_kernel(index_ref, k_ref, v_ref, own_ref, k_rows, v_rows, sems):
    there, upper = slot_rows(index_ref[0])
    copies = [
        pltpu.make_async_copy(k_ref.at[there, :], k_rows, sems.at[0]),
        pltpu.make_async_copy(v_ref.at[there, :], v_rows, sems.at[1]),
    ]
    for copy in copies:
        copy.start()
    for copy in copies:
        copy.wait()
    k = k_rows[...].astype(F32)
    v = v_rows[...].astype(F32)
    k = jnp.where(upper, k[SUMMARY:], k[:SUMMARY])
    v = jnp.where(upper, v[SUMMARY:], v[:SUMMARY])
    own_ref[...] = jnp.concatenate([k, v], axis=0).astype(BF16)


def gather_kernel(*refs):
    *parts, out_ref = refs
    for at, part in enumerate(parts):
        out_ref[at * PAIR : (at + 1) * PAIR, :] = part[...]


def share_kernel(even_ref, came_ref, *out_refs):
    for at, out_ref in enumerate(out_refs):
        mine = even_ref[(at + 1) * PAIR : (at + 2) * PAIR, :].astype(F32)
        came = came_ref[at * PAIR : (at + 1) * PAIR, :].astype(F32)
        out_ref[...] = (mine + came).astype(BF16)


def local_kernel(first, q_ref, k_ref, v_ref, g_ref, w_ref, da_ref, s_ref, dp_ref):
    rows = g_ref.shape[0]
    heads = da_ref.shape[1] // HEAD_DIM
    causal = lax.broadcasted_iota(jnp.int32, (rows, rows), 0) <= lax.broadcasted_iota(
        jnp.int32, (rows, rows), 1
    )
    start = first * HEAD_DIM
    turned = dot(w_ref[start : start + heads * HEAD_DIM, :], g_ref[...], NT).astype(BF16)
    da_ref[...] = turned.T
    for head in range(heads):
        cols = head_cols(first + head)
        s_loc = dot(k_ref[:, cols], q_ref[:, cols], NT) * SCALE
        s_ref[head] = jnp.where(causal, s_loc, -jnp.inf)
        dp_ref[head] = dot(v_ref[:, cols], turned[head_cols(head)], NN)


def head_cols(head):
    return slice(head * HEAD_DIM, (head + 1) * HEAD_DIM)


def of_head(refs, head):
    for ref in refs:
        if head < ref.shape[0]:
            return ref[head]
        head -= ref.shape[0]


def part_cols(refs, head):
    for ref in refs:
        if head < ref.shape[1] // HEAD_DIM:
            return ref[:, head_cols(head)]
        head -= ref.shape[1] // HEAD_DIM


def stacked(refs, cols):
    return jnp.concatenate([ref[:, cols] for ref in refs], axis=0)


def seen(place, slots, rows):
    block = lax.broadcasted_iota(jnp.int32, (slots, rows), 0) // SUMMARY
    half = slots // SUMMARY // 2
    mask = jnp.where(block < half, 2 * block, 2 * (block - half) + 1)
    return (mask ^ place) < place


def attend_kernel(parts, q_ref, v_ref, *rest):
    *ins, attn_ref, p_ref, ds_ref, even_ref, next_ref, odd_ref, sum_ref = rest
    s_refs, dp_refs, da_refs = ins[:parts], ins[parts : 2 * parts], ins[2 * parts : 3 * parts]
    pieces = ins[3 * parts :]
    place = lax.axis_index("ctx")
    rows = q_ref.shape[0]
    heads = q_ref.shape[1] // HEAD_DIM
    half = even_ref.shape[0]
    blocks = 2 * half // PAIR
    slots = blocks * SUMMARY
    visible = seen(place, slots, rows)
    empty = jnp.zeros((blocks, SUMMARY, rows), F32)
    for head in range(heads):
        cols = head_cols(head)
        both = stacked(pieces, cols)
        s_sum = dot(both, q_ref[:, cols], NT).reshape(blocks, PAIR, rows)
        dp_sum = dot(both, part_cols(da_refs, head), NT).reshape(blocks, PAIR, rows)
        sum_ref[head, 0] = s_sum[:, :SUMMARY].reshape(slots, rows)
        sum_ref[head, 1] = dp_sum[:, SUMMARY:].reshape(slots, rows)
    for head in range(heads):
        s_loc = of_head(s_refs, head)
        s_sum = jnp.where(visible, sum_ref[head, 0] * SCALE, -jnp.inf)
        top = jnp.maximum(
            jnp.max(s_loc, axis=0, keepdims=True), jnp.max(s_sum, axis=0, keepdims=True)
        )
        e_loc = jnp.exp(s_loc - top)
        e_sum = jnp.exp(s_sum - top)
        total = jnp.sum(e_loc, axis=0, keepdims=True) + jnp.sum(e_sum, axis=0, keepdims=True)
        share = 1.0 / total
        p_loc = e_loc * share
        p_sum = e_sum * share
        dp_loc = of_head(dp_refs, head)
        dp_sum = sum_ref[head, 1]
        delta = jnp.sum(p_loc * dp_loc, axis=0, keepdims=True) + jnp.sum(
            p_sum * dp_sum, axis=0, keepdims=True
        )
        ds_loc = p_loc * (dp_loc - delta)
        ds_sum = (p_sum * (dp_sum - delta)).reshape(blocks, SUMMARY, rows)
        at_vals = jnp.concatenate([empty, p_sum.reshape(blocks, SUMMARY, rows)], axis=1)
        at_keys = jnp.concatenate([ds_sum, empty], axis=1)
        p_ref[head, :rows, :] = p_loc.astype(BF16)
        p_ref[head, rows:, :] = at_vals.reshape(blocks * PAIR, rows).astype(BF16)
        ds_ref[head, :rows, :] = ds_loc.astype(BF16)
        ds_ref[head, rows:, :] = at_keys.reshape(blocks * PAIR, rows).astype(BF16)
    for head in range(heads):
        cols = head_cols(head)
        term = dot(ds_ref[head, rows:, :], q_ref[:, cols], NN) * SCALE
        term += dot(p_ref[head, rows:, :], part_cols(da_refs, head), NN)
        even_ref[:, cols] = term[:half].astype(BF16)
        next_ref[:, cols] = term[half : half + PAIR].astype(BF16)
        odd_ref[:, cols] = term[half + PAIR :].astype(BF16)
    for head in range(heads):
        cols = head_cols(head)
        values = jnp.concatenate([v_ref[:, cols], stacked(pieces, cols)], axis=0)
        attn_ref[:, cols] = dot(p_ref[head], values, TN).astype(BF16)


def input_grad_kernel(parts, index_ref, q_ref, k_ref, p_ref, ds_ref, *rest):
    *ins, gk_out, gv_out, dq_ref, k_rows, v_rows, dk_ref, dv_ref, gk_ref, gv_ref, sems = rest
    da_refs, pieces = ins[:parts], ins[parts:]
    heads = q_ref.shape[1] // HEAD_DIM
    rows = q_ref.shape[0]
    for head in range(heads):
        cols = head_cols(head)
        dk_ref[:, cols] = dot(ds_ref[head, :rows, :], q_ref[:, cols], NN) * SCALE
        dv_ref[:, cols] = dot(p_ref[head, :rows, :], part_cols(da_refs, head), NN)
    gk_ref[...] = dk_ref[...].astype(BF16)
    gv_ref[...] = dv_ref[...].astype(BF16)
    stores = [
        pltpu.make_async_copy(gk_ref, gk_out, sems.at[1]),
        pltpu.make_async_copy(gv_ref, gv_out, sems.at[2]),
    ]
    for store in stores:
        store.start()
    for head in range(heads):
        cols = head_cols(head)
        keys = jnp.concatenate([k_ref[:, cols], stacked(pieces, cols)], axis=0)
        dq_ref[:, cols] = (dot(ds_ref[head], keys, TN) * SCALE).astype(BF16)
    there, upper = slot_rows(index_ref[0])
    k_rows[...] = dk_ref[there, :]
    v_rows[...] = dv_ref[there, :]
    for store in stores:
        store.wait()


def project_kernel(mask, carried, attn_ref, w_ref, *rest):
    out_refs = rest[carried : len(rest) - carried]
    width = attn_ref.shape[1]
    start = pl.multiple_of((lax.axis_index("head") ^ mask) * width, HEAD_DIM)
    out = dot(attn_ref[...], w_ref[:, pl.ds(start, width)], NN).astype(BF16)
    each = width // len(out_refs)
    for at, out_ref in enumerate(out_refs):
        out_ref[...] = out[:, at * each : (at + 1) * each]


def join_kernel(keep_ref, *rest):
    *came_refs, out_ref = rest
    each = came_refs[0].shape[1]
    for at, came_ref in enumerate(came_refs):
        cols = slice(at * each, (at + 1) * each)
        out_ref[:, cols] = (keep_ref[:, cols].astype(F32) + came_ref[...].astype(F32)).astype(BF16)


def final_kernel(terms, index_ref, gk_ref, gv_ref, k_rows, v_rows, *rest):
    *ins, gk_out, gv_out, out, k_new, v_new, held, sems = rest
    terms, sums = ins[:terms], ins[terms:]
    there, upper = slot_rows(index_ref[0])
    width = held.shape[1]
    step = width // FINAL_PARTS
    stores = []
    for at in range(FINAL_PARTS):
        cols = slice(at * step, (at + 1) * step)
        total = sums[0][:, cols].astype(F32)
        for part in sums[1:]:
            total = total + part[:, cols].astype(F32)
        held[:, cols] = total.astype(BF16)
        stores.append(pltpu.make_async_copy(held.at[:, cols], out.at[:, cols], sems.at[2 + at]))
        stores[-1].start()
    total = terms[0][:PAIR, :].astype(F32)
    for term in terms[1:]:
        total = total + term[...].astype(F32)
    for at, (rows, add, new, target) in enumerate(
        ((k_rows, total[:SUMMARY], k_new, gk_out), (v_rows, total[SUMMARY:], v_new, gv_out))
    ):
        low = jnp.where(upper, 0.0, add)
        high = jnp.where(upper, add, 0.0)
        new[...] = (rows[...] + jnp.concatenate([low, high], axis=0)).astype(BF16)
        stores.append(pltpu.make_async_copy(new, target.at[there, :], sems.at[at]))
        stores[-1].start()
    for store in stores:
        store.wait()


def on_device(queries, key_rows, value_rows, summary_index, out_weight, out_grad):
    rows, width = queries.shape
    heads = width // HEAD_DIM
    shards = lax.axis_size("ctx")
    ranks = lax.axis_size("head")
    half = shards // 2 * PAIR
    slots = shards * SUMMARY
    depth = out_weight.shape[1]
    tall = rows + shards * PAIR

    whole = ((rows, width), BF16)
    rows_held = pltpu.VMEM((PAIR, width), BF16)
    (own,) = call(
        pick_kernel,
        [((PAIR, width), BF16)],
        summary_index, key_rows, value_rows,
        smem=1, hbm=2, flops=8 * 10**9,
        scratch=[rows_held, rows_held, pltpu.SemaphoreType.DMA((2,))],
    )
    evens = [swap(own, "ctx", mask) for mask in range(2, shards, 2)]

    def local(first, count):
        return call(
            functools.partial(local_kernel, first),
            [((rows, count * HEAD_DIM), BF16)]
            + [((count, rows, rows), F32)] * 2,
            queries, key_rows, value_rows, out_grad, out_weight,
            flops=6 * rows * width * depth, moved=width * depth,
        )

    def across(blocks, after):
        (joint,) = call(
            gather_kernel, [((len(blocks) * PAIR, width), BF16)], *blocks, flops=1, moved=1, after=after
        )
        return [joint, swap(joint, "ctx", 1)]

    das, scores, dps, pieces = [], [], [], []
    ends = [max(heads // 3, 1), heads]
    first = 0
    for turn, end in enumerate(ends):
        da, score, dp = local(first, end - first)
        das.append(da)
        scores.append(score)
        dps.append(dp)
        first = end
        if turn == 0:
            pieces = [own, across(evens, (da,))]
    beside = swap(own, "ctx", 1)
    pieces = [own, pieces[1][0], beside, pieces[1][1]]
    parts = len(das)

    small = 2 * heads * tall * rows * HEAD_DIM
    attn, probs, ds, terms, beside, odds = call(
        functools.partial(attend_kernel, parts),
        [whole] + [((heads, tall, rows), BF16)] * 2
        + [((half, width), BF16), ((PAIR, width), BF16), ((half - PAIR, width), BF16)],
        queries, value_rows, *scores, *dps, *das, *pieces,
        scratch=[pltpu.VMEM((heads, 2, slots, rows), F32)],
        flops=8 * small,
    )

    def project(mask, cuts=1, carried=(), after=()):
        cuts = cuts if width % (cuts * HEAD_DIM) == 0 else 1
        return call(
            functools.partial(project_kernel, mask, len(carried)),
            [((rows, width // cuts), BF16)] * cuts + [(x.shape, x.dtype) for x in carried],
            attn, out_weight, *carried,
            alias={2 + at: cuts + at for at in range(len(carried))},
            flops=1, moved=1, after=after,
        )

    def exchanged(mask, cuts):
        sends = [swap(send, "head", 1) for send in project(mask ^ 1, cuts)]
        return [*project(mask), *sends]

    came = []
    for mask in range(2, ranks, 2):
        keep, *sends = exchanged(mask, 3)
        (joined,) = call(join_kernel, [whole], keep, *sends)
        came.append(swap(joined, "head", mask))

    shared = call(
        share_kernel,
        [((PAIR, width), BF16)] * (shards // 2 - 1),
        terms, swap(odds, "ctx", 1),
        flops=5 * 10**10,
    )
    returned = [swap(term, "ctx", 2 * at + 2) for at, term in enumerate(shared)]
    send, beside = project(1, carried=(beside,), after=(shared[0],))
    (keep,) = project(0, after=(returned[0],))
    returned.append(swap(beside, "ctx", 1))
    sends = [swap(send, "head", 1)]
    came = [keep, *sends, *came]
    wide = pltpu.VMEM((rows, width), F32)
    slim = pltpu.VMEM((rows, width), BF16)
    grad_key, grad_value, grad_query, k_rows, v_rows = call(
        functools.partial(input_grad_kernel, parts),
        [whole, whole, whole, ((PAIR, width), F32), ((PAIR, width), F32)],
        summary_index, queries, key_rows, probs, ds, *das, *pieces,
        smem=1, hbm_outs=2, flops=8 * small,
        scratch=[wide, wide, slim, slim, pltpu.SemaphoreType.DMA((3,))],
    )
    patch = pltpu.VMEM((PAIR, width), BF16)
    grad_key, grad_value, attended = call(
        functools.partial(final_kernel, 1 + len(returned)),
        [whole, whole, whole],
        summary_index, grad_key, grad_value, k_rows, v_rows, terms, *returned, *came,
        smem=1, hbm=2, hbm_outs=3, alias={1: 0, 2: 1},
        scratch=[patch, patch, slim, pltpu.SemaphoreType.DMA((2 + FINAL_PARTS,))],
    )
    return (attended, grad_query, grad_key, grad_value)


def solution(mesh):
    return jax.shard_map(
        on_device,
        mesh=mesh,
        in_specs=(
            P("ctx", "head"),
            P("ctx", "head"),
            P("ctx", "head"),
            P("ctx"),
            P("head", None),
            P("ctx", None),
        ),
        out_specs=(P("ctx", "head"), P("ctx", "head"), P("ctx", "head"), P("ctx", "head")),
        check_vma=False,
    )
```

```python
import functools

import jax
import jax.numpy as jnp
from jax import lax
from jax.experimental import pallas as pl
from jax.experimental.pallas import tpu as pltpu
from jax.sharding import PartitionSpec as P

HEAD_DIM = 128
STRIDE = 128
SUMMARY = 8
PAIR = 2 * SUMMARY
FINAL_PARTS = 3
SCALE = HEAD_DIM ** (-0.5)
NT = (((1,), (1,)), ((), ()))
NN = (((1,), (0,)), ((), ()))
TN = (((0,), (0,)), ((), ()))
BF16 = jnp.bfloat16
F32 = jnp.float32
VMEM_LIMIT = 12 * 1024 * 1024


def dot(a, b, dims):
    return lax.dot_general(a, b, dims, preferred_element_type=F32)


def call(
    body, outs, *args, smem=0, hbm=0, hbm_outs=0, alias=None, scratch=(), flops=0, moved=0, after=()
):
    vmem = pl.BlockSpec(memory_space=pltpu.VMEM)
    far = pl.BlockSpec(memory_space=pl.ANY)
    args = [
        pltpu.with_memory_space_constraint(x, pltpu.HBM) if smem <= at < smem + hbm else x
        for at, x in enumerate(args)
    ]
    shapes = [pltpu.HBM(shape, dtype) for shape, dtype in outs[:hbm_outs]]
    shapes += [jax.ShapeDtypeStruct(shape, dtype) for shape, dtype in outs[hbm_outs:]]
    plain = len(args)

    def ordered(*refs):
        body(*refs[:plain], *refs[plain + len(after) :])

    return pl.pallas_call(
        ordered,
        in_specs=[pl.BlockSpec(memory_space=pltpu.SMEM)] * smem
        + [far] * hbm
        + [vmem] * (plain - smem - hbm)
        + [far] * len(after),
        out_specs=[far] * hbm_outs + [vmem] * (len(outs) - hbm_outs),
        out_shape=shapes,
        input_output_aliases=alias or {},
        scratch_shapes=scratch,
        compiler_params=pltpu.CompilerParams(vmem_limit_bytes=VMEM_LIMIT),
        cost_estimate=pl.CostEstimate(flops=flops, bytes_accessed=moved, transcendentals=0),
    )(*args, *after)


def swap(value, axis, mask):
    return lax.ppermute(value, axis, [(i, i ^ mask) for i in range(lax.axis_size(axis))])


def slot_rows(index):
    return pl.ds(pl.multiple_of((index // 2) * PAIR, PAIR), PAIR), index % 2 == 1


def pick_kernel(index_ref, k_ref, v_ref, own_ref, k_rows, v_rows, sems):
    there, upper = slot_rows(index_ref[0])
    copies = [
        pltpu.make_async_copy(k_ref.at[there, :], k_rows, sems.at[0]),
        pltpu.make_async_copy(v_ref.at[there, :], v_rows, sems.at[1]),
    ]
    for copy in copies:
        copy.start()
    for copy in copies:
        copy.wait()
    k = k_rows[...].astype(F32)
    v = v_rows[...].astype(F32)
    k = jnp.where(upper, k[SUMMARY:], k[:SUMMARY])
    v = jnp.where(upper, v[SUMMARY:], v[:SUMMARY])
    own_ref[...] = jnp.concatenate([k, v], axis=0).astype(BF16)


def gather_kernel(*refs):
    *parts, out_ref = refs
    for at, part in enumerate(parts):
        out_ref[at * PAIR : (at + 1) * PAIR, :] = part[...]


def share_kernel(even_ref, came_ref, *out_refs):
    for at, out_ref in enumerate(out_refs):
        mine = even_ref[(at + 1) * PAIR : (at + 2) * PAIR, :].astype(F32)
        came = came_ref[at * PAIR : (at + 1) * PAIR, :].astype(F32)
        out_ref[...] = (mine + came).astype(BF16)


def local_kernel(first, q_ref, k_ref, v_ref, g_ref, w_ref, da_ref, s_ref, dp_ref):
    rows = g_ref.shape[0]
    heads = da_ref.shape[1] // HEAD_DIM
    causal = lax.broadcasted_iota(jnp.int32, (rows, rows), 0) <= lax.broadcasted_iota(
        jnp.int32, (rows, rows), 1
    )
    for head in range(heads):
        cols = head_cols(first + head)
        s_loc = dot(k_ref[:, cols], q_ref[:, cols], NT) * SCALE
        s_ref[head] = jnp.where(causal, s_loc, -jnp.inf)
    start = first * HEAD_DIM
    turned = dot(w_ref[start : start + heads * HEAD_DIM, :], g_ref[...], NT).astype(BF16)
    da_ref[...] = turned.T
    for head in range(heads):
        dp_ref[head] = dot(v_ref[:, head_cols(first + head)], turned[head_cols(head)], NN)


def head_cols(head):
    return slice(head * HEAD_DIM, (head + 1) * HEAD_DIM)


def of_head(refs, head):
    for ref in refs:
        if head < ref.shape[0]:
            return ref[head]
        head -= ref.shape[0]


def part_cols(refs, head):
    for ref in refs:
        if head < ref.shape[1] // HEAD_DIM:
            return ref[:, head_cols(head)]
        head -= ref.shape[1] // HEAD_DIM


def stacked(refs, cols):
    return jnp.concatenate([ref[:, cols] for ref in refs], axis=0)


def seen(place, slots, rows):
    block = lax.broadcasted_iota(jnp.int32, (slots, rows), 0) // SUMMARY
    half = slots // SUMMARY // 2
    mask = jnp.where(block < half, 2 * block, 2 * (block - half) + 1)
    return (mask ^ place) < place


def attend_kernel(parts, q_ref, v_ref, *rest):
    *ins, attn_ref, p_ref, ds_ref, even_ref, next_ref, odd_ref, sum_ref = rest
    s_refs, dp_refs, da_refs = ins[:parts], ins[parts : 2 * parts], ins[2 * parts : 3 * parts]
    pieces = ins[3 * parts :]
    place = lax.axis_index("ctx")
    rows = q_ref.shape[0]
    heads = q_ref.shape[1] // HEAD_DIM
    half = even_ref.shape[0]
    blocks = 2 * half // PAIR
    slots = blocks * SUMMARY
    visible = seen(place, slots, rows)
    empty = jnp.zeros((blocks, SUMMARY, rows), F32)
    for head in range(heads):
        cols = head_cols(head)
        both = stacked(pieces, cols)
        s_sum = dot(both, q_ref[:, cols], NT).reshape(blocks, PAIR, rows)
        dp_sum = dot(both, part_cols(da_refs, head), NT).reshape(blocks, PAIR, rows)
        sum_ref[head, 0] = s_sum[:, :SUMMARY].reshape(slots, rows)
        sum_ref[head, 1] = dp_sum[:, SUMMARY:].reshape(slots, rows)
    for head in range(heads):
        s_loc = of_head(s_refs, head)
        s_sum = jnp.where(visible, sum_ref[head, 0] * SCALE, -jnp.inf)
        top = jnp.maximum(
            jnp.max(s_loc, axis=0, keepdims=True), jnp.max(s_sum, axis=0, keepdims=True)
        )
        e_loc = jnp.exp(s_loc - top)
        e_sum = jnp.exp(s_sum - top)
        total = jnp.sum(e_loc, axis=0, keepdims=True) + jnp.sum(e_sum, axis=0, keepdims=True)
        share = 1.0 / total
        p_loc = e_loc * share
        p_sum = e_sum * share
        dp_loc = of_head(dp_refs, head)
        dp_sum = sum_ref[head, 1]
        delta = jnp.sum(p_loc * dp_loc, axis=0, keepdims=True) + jnp.sum(
            p_sum * dp_sum, axis=0, keepdims=True
        )
        ds_loc = p_loc * (dp_loc - delta)
        ds_sum = (p_sum * (dp_sum - delta)).reshape(blocks, SUMMARY, rows)
        at_vals = jnp.concatenate([empty, p_sum.reshape(blocks, SUMMARY, rows)], axis=1)
        at_keys = jnp.concatenate([ds_sum, empty], axis=1)
        p_ref[head, :rows, :] = p_loc.astype(BF16)
        p_ref[head, rows:, :] = at_vals.reshape(blocks * PAIR, rows).astype(BF16)
        ds_ref[head, :rows, :] = ds_loc.astype(BF16)
        ds_ref[head, rows:, :] = at_keys.reshape(blocks * PAIR, rows).astype(BF16)
    for head in range(heads):
        cols = head_cols(head)
        term = dot(ds_ref[head, rows:, :], q_ref[:, cols], NN) * SCALE
        term += dot(p_ref[head, rows:, :], part_cols(da_refs, head), NN)
        even_ref[:, cols] = term[:half].astype(BF16)
        next_ref[:, cols] = term[half : half + PAIR].astype(BF16)
        odd_ref[:, cols] = term[half + PAIR :].astype(BF16)
    for head in range(heads):
        cols = head_cols(head)
        values = jnp.concatenate([v_ref[:, cols], stacked(pieces, cols)], axis=0)
        attn_ref[:, cols] = dot(p_ref[head], values, TN).astype(BF16)


def input_grad_kernel(parts, index_ref, q_ref, k_ref, p_ref, ds_ref, *rest):
    *ins, gk_out, gv_out, dq_ref, k_rows, v_rows, dk_ref, dv_ref, gk_ref, gv_ref, sems = rest
    da_refs, pieces = ins[:parts], ins[parts:]
    heads = q_ref.shape[1] // HEAD_DIM
    rows = q_ref.shape[0]
    for head in range(heads):
        cols = head_cols(head)
        dk_ref[:, cols] = dot(ds_ref[head, :rows, :], q_ref[:, cols], NN) * SCALE
        dv_ref[:, cols] = dot(p_ref[head, :rows, :], part_cols(da_refs, head), NN)
    gk_ref[...] = dk_ref[...].astype(BF16)
    gv_ref[...] = dv_ref[...].astype(BF16)
    stores = [
        pltpu.make_async_copy(gk_ref, gk_out, sems.at[1]),
        pltpu.make_async_copy(gv_ref, gv_out, sems.at[2]),
    ]
    for store in stores:
        store.start()
    for head in range(heads):
        cols = head_cols(head)
        keys = jnp.concatenate([k_ref[:, cols], stacked(pieces, cols)], axis=0)
        dq_ref[:, cols] = (dot(ds_ref[head], keys, TN) * SCALE).astype(BF16)
    there, upper = slot_rows(index_ref[0])
    k_rows[...] = dk_ref[there, :]
    v_rows[...] = dv_ref[there, :]
    for store in stores:
        store.wait()


def project_kernel(mask, carried, attn_ref, w_ref, *rest):
    out_refs = rest[carried : len(rest) - carried]
    width = attn_ref.shape[1]
    start = pl.multiple_of((lax.axis_index("head") ^ mask) * width, HEAD_DIM)
    out = dot(attn_ref[...], w_ref[:, pl.ds(start, width)], NN).astype(BF16)
    each = width // len(out_refs)
    for at, out_ref in enumerate(out_refs):
        out_ref[...] = out[:, at * each : (at + 1) * each]


def join_kernel(keep_ref, *rest):
    *came_refs, out_ref = rest
    each = came_refs[0].shape[1]
    for at, came_ref in enumerate(came_refs):
        cols = slice(at * each, (at + 1) * each)
        out_ref[:, cols] = (keep_ref[:, cols].astype(F32) + came_ref[...].astype(F32)).astype(BF16)


def final_kernel(terms, index_ref, gk_ref, gv_ref, k_rows, v_rows, *rest):
    *ins, gk_out, gv_out, out, k_new, v_new, held, sems = rest
    terms, sums = ins[:terms], ins[terms:]
    there, upper = slot_rows(index_ref[0])
    width = held.shape[1]
    step = width // FINAL_PARTS
    stores = []
    for at in range(FINAL_PARTS):
        cols = slice(at * step, (at + 1) * step)
        total = sums[0][:, cols].astype(F32)
        for part in sums[1:]:
            total = total + part[:, cols].astype(F32)
        held[:, cols] = total.astype(BF16)
        stores.append(pltpu.make_async_copy(held.at[:, cols], out.at[:, cols], sems.at[2 + at]))
        stores[-1].start()
    total = terms[0][:PAIR, :].astype(F32)
    for term in terms[1:]:
        total = total + term[...].astype(F32)
    for at, (rows, add, new, target) in enumerate(
        ((k_rows, total[:SUMMARY], k_new, gk_out), (v_rows, total[SUMMARY:], v_new, gv_out))
    ):
        low = jnp.where(upper, 0.0, add)
        high = jnp.where(upper, add, 0.0)
        new[...] = (rows[...] + jnp.concatenate([low, high], axis=0)).astype(BF16)
        stores.append(pltpu.make_async_copy(new, target.at[there, :], sems.at[at]))
        stores[-1].start()
    for store in stores:
        store.wait()


def on_device(queries, key_rows, value_rows, summary_index, out_weight, out_grad):
    rows, width = queries.shape
    heads = width // HEAD_DIM
    shards = lax.axis_size("ctx")
    ranks = lax.axis_size("head")
    half = shards // 2 * PAIR
    slots = shards * SUMMARY
    depth = out_weight.shape[1]
    tall = rows + shards * PAIR

    whole = ((rows, width), BF16)
    rows_held = pltpu.VMEM((PAIR, width), BF16)
    (own,) = call(
        pick_kernel,
        [((PAIR, width), BF16)],
        summary_index, key_rows, value_rows,
        smem=1, hbm=2, flops=8 * 10**9,
        scratch=[rows_held, rows_held, pltpu.SemaphoreType.DMA((2,))],
    )
    evens = [swap(own, "ctx", mask) for mask in range(2, shards, 2)]

    def local(first, count):
        return call(
            functools.partial(local_kernel, first),
            [((rows, count * HEAD_DIM), BF16)]
            + [((count, rows, rows), F32)] * 2,
            queries, key_rows, value_rows, out_grad, out_weight,
            flops=6 * rows * width * depth, moved=width * depth,
        )

    def across(blocks, after):
        (joint,) = call(
            gather_kernel, [((len(blocks) * PAIR, width), BF16)], *blocks, flops=1, moved=1, after=after
        )
        return [joint, swap(joint, "ctx", 1)]

    das, scores, dps, pieces = [], [], [], []
    ends = [max(heads // 3, 1), heads]
    first = 0
    for turn, end in enumerate(ends):
        da, score, dp = local(first, end - first)
        das.append(da)
        scores.append(score)
        dps.append(dp)
        first = end
        if turn == 0:
            pieces = [own, across(evens, (da,))]
    beside = swap(own, "ctx", 1)
    pieces = [own, pieces[1][0], beside, pieces[1][1]]
    parts = len(das)

    small = 2 * heads * tall * rows * HEAD_DIM
    attn, probs, ds, terms, beside, odds = call(
        functools.partial(attend_kernel, parts),
        [whole] + [((heads, tall, rows), BF16)] * 2
        + [((half, width), BF16), ((PAIR, width), BF16), ((half - PAIR, width), BF16)],
        queries, value_rows, *scores, *dps, *das, *pieces,
        scratch=[pltpu.VMEM((heads, 2, slots, rows), F32)],
        flops=8 * small,
    )

    def project(mask, cuts=1, carried=(), after=()):
        cuts = cuts if width % (cuts * HEAD_DIM) == 0 else 1
        return call(
            functools.partial(project_kernel, mask, len(carried)),
            [((rows, width // cuts), BF16)] * cuts + [(x.shape, x.dtype) for x in carried],
            attn, out_weight, *carried,
            alias={2 + at: cuts + at for at in range(len(carried))},
            flops=1, moved=1, after=after,
        )

    def exchanged(mask, cuts):
        sends = [swap(send, "head", 1) for send in project(mask ^ 1, cuts)]
        return [*project(mask), *sends]

    came = []
    for mask in range(2, ranks, 2):
        keep, *sends = exchanged(mask, 3)
        (joined,) = call(join_kernel, [whole], keep, *sends)
        came.append(swap(joined, "head", mask))

    shared = call(
        share_kernel,
        [((PAIR, width), BF16)] * (shards // 2 - 1),
        terms, swap(odds, "ctx", 1),
        flops=5 * 10**10,
    )
    returned = [swap(term, "ctx", 2 * at + 2) for at, term in enumerate(shared)]
    send, beside = project(1, carried=(beside,), after=(shared[0],))
    (keep,) = project(0, after=(returned[0],))
    returned.append(swap(beside, "ctx", 1))
    sends = [swap(send, "head", 1)]
    came = [keep, *sends, *came]
    wide = pltpu.VMEM((rows, width), F32)
    slim = pltpu.VMEM((rows, width), BF16)
    grad_key, grad_value, grad_query, k_rows, v_rows = call(
        functools.partial(input_grad_kernel, parts),
        [whole, whole, whole, ((PAIR, width), F32), ((PAIR, width), F32)],
        summary_index, queries, key_rows, probs, ds, *das, *pieces,
        smem=1, hbm_outs=2, flops=8 * small,
        scratch=[wide, wide, slim, slim, pltpu.SemaphoreType.DMA((3,))],
    )
    patch = pltpu.VMEM((PAIR, width), BF16)
    grad_key, grad_value, attended = call(
        functools.partial(final_kernel, 1 + len(returned)),
        [whole, whole, whole],
        summary_index, grad_key, grad_value, k_rows, v_rows, terms, *returned, *came,
        smem=1, hbm=2, hbm_outs=3, alias={1: 0, 2: 1},
        scratch=[patch, patch, slim, pltpu.SemaphoreType.DMA((2 + FINAL_PARTS,))],
    )
    return (attended, grad_query, grad_key, grad_value)


def solution(mesh):
    return jax.shard_map(
        on_device,
        mesh=mesh,
        in_specs=(
            P("ctx", "head"),
            P("ctx", "head"),
            P("ctx", "head"),
            P("ctx"),
            P("head", None),
            P("ctx", None),
        ),
        out_specs=(P("ctx", "head"), P("ctx", "head"), P("ctx", "head"), P("ctx", "head")),
        check_vma=False,
    )
```

```python
import functools

import jax
import jax.numpy as jnp
from jax import lax
from jax.experimental import pallas as pl
from jax.experimental.pallas import tpu as pltpu
from jax.sharding import PartitionSpec as P

HEAD_DIM = 128
STRIDE = 128
SUMMARY = 8
PAIR = 2 * SUMMARY
FINAL_PARTS = 3
SCALE = HEAD_DIM ** (-0.5)
NT = (((1,), (1,)), ((), ()))
NN = (((1,), (0,)), ((), ()))
TN = (((0,), (0,)), ((), ()))
BF16 = jnp.bfloat16
F32 = jnp.float32
VMEM_LIMIT = 12 * 1024 * 1024


def dot(a, b, dims):
    return lax.dot_general(a, b, dims, preferred_element_type=F32)


def call(
    body, outs, *args, smem=0, hbm=0, hbm_outs=0, alias=None, scratch=(), flops=0, moved=0, after=()
):
    vmem = pl.BlockSpec(memory_space=pltpu.VMEM)
    far = pl.BlockSpec(memory_space=pl.ANY)
    args = [
        pltpu.with_memory_space_constraint(x, pltpu.HBM) if smem <= at < smem + hbm else x
        for at, x in enumerate(args)
    ]
    shapes = [pltpu.HBM(shape, dtype) for shape, dtype in outs[:hbm_outs]]
    shapes += [jax.ShapeDtypeStruct(shape, dtype) for shape, dtype in outs[hbm_outs:]]
    plain = len(args)

    def ordered(*refs):
        body(*refs[:plain], *refs[plain + len(after) :])

    return pl.pallas_call(
        ordered,
        in_specs=[pl.BlockSpec(memory_space=pltpu.SMEM)] * smem
        + [far] * hbm
        + [vmem] * (plain - smem - hbm)
        + [far] * len(after),
        out_specs=[far] * hbm_outs + [vmem] * (len(outs) - hbm_outs),
        out_shape=shapes,
        input_output_aliases=alias or {},
        scratch_shapes=scratch,
        compiler_params=pltpu.CompilerParams(vmem_limit_bytes=VMEM_LIMIT),
        cost_estimate=pl.CostEstimate(flops=flops, bytes_accessed=moved, transcendentals=0),
    )(*args, *after)


def swap(value, axis, mask):
    return lax.ppermute(value, axis, [(i, i ^ mask) for i in range(lax.axis_size(axis))])


def slot_rows(index):
    return pl.ds(pl.multiple_of((index // 2) * PAIR, PAIR), PAIR), index % 2 == 1


def pick_kernel(index_ref, k_ref, v_ref, own_ref, k_rows, v_rows, sems):
    there, upper = slot_rows(index_ref[0])
    copies = [
        pltpu.make_async_copy(k_ref.at[there, :], k_rows, sems.at[0]),
        pltpu.make_async_copy(v_ref.at[there, :], v_rows, sems.at[1]),
    ]
    for copy in copies:
        copy.start()
    for copy in copies:
        copy.wait()
    k = k_rows[...].astype(F32)
    v = v_rows[...].astype(F32)
    k = jnp.where(upper, k[SUMMARY:], k[:SUMMARY])
    v = jnp.where(upper, v[SUMMARY:], v[:SUMMARY])
    own_ref[...] = jnp.concatenate([k, v], axis=0).astype(BF16)


def gather_kernel(*refs):
    *parts, out_ref = refs
    for at, part in enumerate(parts):
        out_ref[at * PAIR : (at + 1) * PAIR, :] = part[...]


def share_kernel(even_ref, came_ref, *out_refs):
    for at, out_ref in enumerate(out_refs):
        mine = even_ref[(at + 1) * PAIR : (at + 2) * PAIR, :].astype(F32)
        came = came_ref[at * PAIR : (at + 1) * PAIR, :].astype(F32)
        out_ref[...] = (mine + came).astype(BF16)


def local_kernel(first, q_ref, k_ref, v_ref, g_ref, w_ref, da_ref, s_ref, dp_ref):
    rows = g_ref.shape[0]
    heads = da_ref.shape[1] // HEAD_DIM
    causal = lax.broadcasted_iota(jnp.int32, (rows, rows), 0) <= lax.broadcasted_iota(
        jnp.int32, (rows, rows), 1
    )
    start = first * HEAD_DIM
    turned = dot(w_ref[start : start + heads * HEAD_DIM, :], g_ref[...], NT).astype(BF16)
    da_ref[...] = turned.T
    for head in range(heads):
        cols = head_cols(first + head)
        s_loc = dot(k_ref[:, cols], q_ref[:, cols], NT) * SCALE
        s_ref[head] = jnp.where(causal, s_loc, -jnp.inf)
        dp_ref[head] = dot(v_ref[:, cols], turned[head_cols(head)], NN)


def head_cols(head):
    return slice(head * HEAD_DIM, (head + 1) * HEAD_DIM)


def of_head(refs, head):
    for ref in refs:
        if head < ref.shape[0]:
            return ref[head]
        head -= ref.shape[0]


def part_cols(refs, head):
    for ref in refs:
        if head < ref.shape[1] // HEAD_DIM:
            return ref[:, head_cols(head)]
        head -= ref.shape[1] // HEAD_DIM


def stacked(refs, cols):
    return jnp.concatenate([ref[:, cols] for ref in refs], axis=0)


def seen(place, slots, rows):
    block = lax.broadcasted_iota(jnp.int32, (slots, rows), 0) // SUMMARY
    half = slots // SUMMARY // 2
    mask = jnp.where(block < half, 2 * block, 2 * (block - half) + 1)
    return (mask ^ place) < place


def attend_kernel(parts, q_ref, v_ref, *rest):
    *ins, attn_ref, p_ref, ds_ref, even_ref, next_ref, odd_ref, sum_ref = rest
    s_refs, dp_refs, da_refs = ins[:parts], ins[parts : 2 * parts], ins[2 * parts : 3 * parts]
    pieces = ins[3 * parts :]
    place = lax.axis_index("ctx")
    rows = q_ref.shape[0]
    heads = q_ref.shape[1] // HEAD_DIM
    half = even_ref.shape[0]
    blocks = 2 * half // PAIR
    slots = blocks * SUMMARY
    visible = seen(place, slots, rows)
    empty = jnp.zeros((blocks, SUMMARY, rows), F32)
    for head in range(heads):
        cols = head_cols(head)
        both = stacked(pieces, cols)
        s_sum = dot(both, q_ref[:, cols], NT).reshape(blocks, PAIR, rows)
        dp_sum = dot(both, part_cols(da_refs, head), NT).reshape(blocks, PAIR, rows)
        sum_ref[head, 0] = s_sum[:, :SUMMARY].reshape(slots, rows)
        sum_ref[head, 1] = dp_sum[:, SUMMARY:].reshape(slots, rows)
    for head in range(heads):
        s_loc = of_head(s_refs, head)
        s_sum = jnp.where(visible, sum_ref[head, 0] * SCALE, -jnp.inf)
        top = jnp.maximum(
            jnp.max(s_loc, axis=0, keepdims=True), jnp.max(s_sum, axis=0, keepdims=True)
        )
        e_loc = jnp.exp(s_loc - top)
        e_sum = jnp.exp(s_sum - top)
        total = jnp.sum(e_loc, axis=0, keepdims=True) + jnp.sum(e_sum, axis=0, keepdims=True)
        share = 1.0 / total
        p_loc = e_loc * share
        p_sum = e_sum * share
        dp_loc = of_head(dp_refs, head)
        dp_sum = sum_ref[head, 1]
        delta = jnp.sum(p_loc * dp_loc, axis=0, keepdims=True) + jnp.sum(
            p_sum * dp_sum, axis=0, keepdims=True
        )
        ds_loc = p_loc * (dp_loc - delta)
        ds_sum = (p_sum * (dp_sum - delta)).reshape(blocks, SUMMARY, rows)
        at_vals = jnp.concatenate([empty, p_sum.reshape(blocks, SUMMARY, rows)], axis=1)
        at_keys = jnp.concatenate([ds_sum, empty], axis=1)
        p_ref[head, :rows, :] = p_loc.astype(BF16)
        p_ref[head, rows:, :] = at_vals.reshape(blocks * PAIR, rows).astype(BF16)
        ds_ref[head, :rows, :] = ds_loc.astype(BF16)
        ds_ref[head, rows:, :] = at_keys.reshape(blocks * PAIR, rows).astype(BF16)
    for head in range(heads):
        cols = head_cols(head)
        term = dot(ds_ref[head, rows:, :], q_ref[:, cols], NN) * SCALE
        term += dot(p_ref[head, rows:, :], part_cols(da_refs, head), NN)
        even_ref[:, cols] = term[:half].astype(BF16)
        next_ref[:, cols] = term[half : half + PAIR].astype(BF16)
        odd_ref[:, cols] = term[half + PAIR :].astype(BF16)
    for head in range(heads):
        cols = head_cols(head)
        values = jnp.concatenate([v_ref[:, cols], stacked(pieces, cols)], axis=0)
        attn_ref[:, cols] = dot(p_ref[head], values, TN).astype(BF16)


def input_grad_kernel(parts, index_ref, q_ref, k_ref, p_ref, ds_ref, *rest):
    *ins, gk_out, gv_out, dq_ref, k_rows, v_rows, dk_ref, dv_ref, gk_ref, gv_ref, sems = rest
    da_refs, pieces = ins[:parts], ins[parts:]
    heads = q_ref.shape[1] // HEAD_DIM
    rows = q_ref.shape[0]
    for head in range(heads):
        cols = head_cols(head)
        dk_ref[:, cols] = dot(ds_ref[head, :rows, :], q_ref[:, cols], NN) * SCALE
        dv_ref[:, cols] = dot(p_ref[head, :rows, :], part_cols(da_refs, head), NN)
    gk_ref[...] = dk_ref[...].astype(BF16)
    gv_ref[...] = dv_ref[...].astype(BF16)
    stores = [
        pltpu.make_async_copy(gk_ref, gk_out, sems.at[1]),
        pltpu.make_async_copy(gv_ref, gv_out, sems.at[2]),
    ]
    for store in stores:
        store.start()
    for head in range(heads):
        cols = head_cols(head)
        keys = jnp.concatenate([k_ref[:, cols], stacked(pieces, cols)], axis=0)
        dq_ref[:, cols] = (dot(ds_ref[head], keys, TN) * SCALE).astype(BF16)
    there, upper = slot_rows(index_ref[0])
    k_rows[...] = dk_ref[there, :]
    v_rows[...] = dv_ref[there, :]
    for store in stores:
        store.wait()


def project_kernel(mask, carried, attn_ref, w_ref, *rest):
    out_refs = rest[carried : len(rest) - carried]
    width = attn_ref.shape[1]
    start = pl.multiple_of((lax.axis_index("head") ^ mask) * width, HEAD_DIM)
    out = dot(attn_ref[...], w_ref[:, pl.ds(start, width)], NN).astype(BF16)
    each = width // len(out_refs)
    for at, out_ref in enumerate(out_refs):
        out_ref[...] = out[:, at * each : (at + 1) * each]


def join_kernel(keep_ref, *rest):
    *came_refs, out_ref = rest
    each = came_refs[0].shape[1]
    for at, came_ref in enumerate(came_refs):
        cols = slice(at * each, (at + 1) * each)
        out_ref[:, cols] = (keep_ref[:, cols].astype(F32) + came_ref[...].astype(F32)).astype(BF16)


def final_kernel(terms, index_ref, gk_ref, gv_ref, k_rows, v_rows, *rest):
    *ins, gk_out, gv_out, out, k_new, v_new, held, sems = rest
    terms, sums = ins[:terms], ins[terms:]
    there, upper = slot_rows(index_ref[0])
    width = held.shape[1]
    step = width // FINAL_PARTS
    stores = []
    for at in range(FINAL_PARTS):
        cols = slice(at * step, (at + 1) * step)
        total = sums[0][:, cols].astype(F32)
        for part in sums[1:]:
            total = total + part[:, cols].astype(F32)
        held[:, cols] = total.astype(BF16)
        stores.append(pltpu.make_async_copy(held.at[:, cols], out.at[:, cols], sems.at[2 + at]))
        stores[-1].start()
    total = terms[0][:PAIR, :].astype(F32)
    for term in terms[1:]:
        total = total + term[...].astype(F32)
    for at, (rows, add, new, target) in enumerate(
        ((k_rows, total[:SUMMARY], k_new, gk_out), (v_rows, total[SUMMARY:], v_new, gv_out))
    ):
        low = jnp.where(upper, 0.0, add)
        high = jnp.where(upper, add, 0.0)
        new[...] = (rows[...] + jnp.concatenate([low, high], axis=0)).astype(BF16)
        stores.append(pltpu.make_async_copy(new, target.at[there, :], sems.at[at]))
        stores[-1].start()
    for store in stores:
        store.wait()


def on_device(queries, key_rows, value_rows, summary_index, out_weight, out_grad):
    rows, width = queries.shape
    heads = width // HEAD_DIM
    shards = lax.axis_size("ctx")
    ranks = lax.axis_size("head")
    half = shards // 2 * PAIR
    slots = shards * SUMMARY
    depth = out_weight.shape[1]
    tall = rows + shards * PAIR

    whole = ((rows, width), BF16)
    rows_held = pltpu.VMEM((PAIR, width), BF16)
    (own,) = call(
        pick_kernel,
        [((PAIR, width), BF16)],
        summary_index, key_rows, value_rows,
        smem=1, hbm=2, flops=8 * 10**9,
        scratch=[rows_held, rows_held, pltpu.SemaphoreType.DMA((2,))],
    )
    evens = [swap(own, "ctx", mask) for mask in range(shards - 2, 0, -2)][::-1]

    def local(first, count):
        return call(
            functools.partial(local_kernel, first),
            [((rows, count * HEAD_DIM), BF16)]
            + [((count, rows, rows), F32)] * 2,
            queries, key_rows, value_rows, out_grad, out_weight,
            flops=6 * rows * width * depth, moved=width * depth,
        )

    def across(blocks, after):
        (joint,) = call(
            gather_kernel, [((len(blocks) * PAIR, width), BF16)], *blocks, flops=1, moved=1, after=after
        )
        return [joint, swap(joint, "ctx", 1)]

    das, scores, dps, pieces = [], [], [], []
    ends = [max(heads // 3, 1), heads]
    first = 0
    for turn, end in enumerate(ends):
        da, score, dp = local(first, end - first)
        das.append(da)
        scores.append(score)
        dps.append(dp)
        first = end
        if turn == 0:
            pieces = [own, across(evens, (da,))]
    beside = swap(own, "ctx", 1)
    pieces = [own, pieces[1][0], beside, pieces[1][1]]
    parts = len(das)

    small = 2 * heads * tall * rows * HEAD_DIM
    attn, probs, ds, terms, beside, odds = call(
        functools.partial(attend_kernel, parts),
        [whole] + [((heads, tall, rows), BF16)] * 2
        + [((half, width), BF16), ((PAIR, width), BF16), ((half - PAIR, width), BF16)],
        queries, value_rows, *scores, *dps, *das, *pieces,
        scratch=[pltpu.VMEM((heads, 2, slots, rows), F32)],
        flops=8 * small,
    )

    def project(mask, cuts=1, carried=(), after=()):
        cuts = cuts if width % (cuts * HEAD_DIM) == 0 else 1
        return call(
            functools.partial(project_kernel, mask, len(carried)),
            [((rows, width // cuts), BF16)] * cuts + [(x.shape, x.dtype) for x in carried],
            attn, out_weight, *carried,
            alias={2 + at: cuts + at for at in range(len(carried))},
            flops=1, moved=1, after=after,
        )

    def exchanged(mask, cuts):
        sends = [swap(send, "head", 1) for send in project(mask ^ 1, cuts)]
        return [*project(mask), *sends]

    came = []
    for mask in range(2, ranks, 2):
        keep, *sends = exchanged(mask, 3)
        (joined,) = call(join_kernel, [whole], keep, *sends)
        came.append(swap(joined, "head", mask))

    shared = call(
        share_kernel,
        [((PAIR, width), BF16)] * (shards // 2 - 1),
        terms, swap(odds, "ctx", 1),
        flops=5 * 10**10,
    )
    returned = [swap(term, "ctx", 2 * at + 2) for at, term in enumerate(shared)]
    send, beside = project(1, carried=(beside,), after=(shared[0],))
    (keep,) = project(0, after=(returned[0],))
    returned.append(swap(beside, "ctx", 1))
    sends = [swap(send, "head", 1)]
    came = [keep, *sends, *came]
    wide = pltpu.VMEM((rows, width), F32)
    slim = pltpu.VMEM((rows, width), BF16)
    grad_key, grad_value, grad_query, k_rows, v_rows = call(
        functools.partial(input_grad_kernel, parts),
        [whole, whole, whole, ((PAIR, width), F32), ((PAIR, width), F32)],
        summary_index, queries, key_rows, probs, ds, *das, *pieces,
        smem=1, hbm_outs=2, flops=8 * small,
        scratch=[wide, wide, slim, slim, pltpu.SemaphoreType.DMA((3,))],
    )
    patch = pltpu.VMEM((PAIR, width), BF16)
    grad_key, grad_value, attended = call(
        functools.partial(final_kernel, 1 + len(returned)),
        [whole, whole, whole],
        summary_index, grad_key, grad_value, k_rows, v_rows, terms, *returned, *came,
        smem=1, hbm=2, hbm_outs=3, alias={1: 0, 2: 1},
        scratch=[patch, patch, slim, pltpu.SemaphoreType.DMA((2 + FINAL_PARTS,))],
    )
    return (attended, grad_query, grad_key, grad_value)


def solution(mesh):
    return jax.shard_map(
        on_device,
        mesh=mesh,
        in_specs=(
            P("ctx", "head"),
            P("ctx", "head"),
            P("ctx", "head"),
            P("ctx"),
            P("head", None),
            P("ctx", None),
        ),
        out_specs=(P("ctx", "head"), P("ctx", "head"), P("ctx", "head"), P("ctx", "head")),
        check_vma=False,
    )
```
